256 devices in a mesh: dom: 16 (over x, y), depth: 16 (over z, core).
Axes of the slice: x: 4, y: 4, z: 8, core: 2. Of those that a mesh axis runs over, the one named last changes fastest.
Arguments:
- head: float32 [16, 1024, 512], P('depth', 'dom'), may hold values from -1.5 to 0.3
- water_prev: float32 [16, 1024, 512], P('depth', 'dom'), may hold values from 0.05 to 0.4
- alpha: float32 [16, 1024, 512], P('depth', 'dom'), may hold values from 0.3 to 3
- shape_n: float32 [16, 1024, 512], P('depth', 'dom'), may hold values from 1.3 to 3
- theta_r: float32 [16, 1024, 512], P('depth', 'dom'), may hold values from 0.02 to 0.1
- theta_s: float32 [16, 1024, 512], P('depth', 'dom'), may hold values from 0.35 to 0.5
- sat_cond: float32 [16, 1024, 512], P('depth', 'dom'), may hold values from 0.5 to 5
- refine: int32 [1024], P('dom'), may hold values from 0 to 8
- destination: int32 [1024], P('dom'), may hold values from 0 to 1023, as said below
- neighbours: int32 [1024, 4, 4], P('dom'), may hold values from -1 to 1023, as said below
Outputs:
- new_head: float32 [16, 1024, 512], P('depth', 'dom')
- residual: float32 [16, 1024, 512], P('depth', 'dom')
The draws below stay inside these ranges and needn't reach their ends.
Inputs may be any that keep to these rules, and one draw needn't show every extreme that they name: destination is a permutation of the 1024 positions, position p on device p // 64. The blocks of each device go to exactly 8 other devices, exactly 4 to each; its other blocks stay on it. neighbours[p, f] lists the new positions beyond lateral face f of new block p: all four entries -1 where there is no neighbour; one block in entry 0 and -1 in the rest for a face of equal size; or four finer blocks, entry (a // 4) * 2 + b // 4 for face cell (a, b). Every listed block lies at most 16 positions from p, some at exactly 16.
All inputs are finite; a program needn't handle non-finite values.
Results may differ from the reference program's by a relative error of at most 0.0003.
Values sent between devices are 32-bit elements; how exact they have to be, the bound alone decides.
No kernel may reach another device: no remote copies, remote signals or barrier semaphores. Data moves between devices by JAX's collectives and lax.ppermute only.
A program may use at most 128 MiB of HBM per device.

```python
import math
import jax
import jax.numpy as jnp
import numpy as np
from jax import lax

CELLS = 512
BLK_DEV = 64
LAYERS = 16
BLOCKS = 1024
GROUPS = 8
CAP = 4
REACH = 16


def draw_destination(key, part):
    key = jax.random.fold_in(key, 11)
    keys = jax.random.split(key, 5)
    owners = BLOCKS // BLK_DEV
    sigma = jax.random.permutation(keys[0], owners)
    inv_sigma = jnp.zeros((owners,), jnp.int32).at[sigma].set(jnp.arange(owners, dtype=jnp.int32))
    shifts = jax.random.permutation(keys[2], owners - 1)[:GROUPS] + 1
    device = jnp.arange(owners)[:, None]
    local = jnp.arange(BLK_DEV)[None, :]
    group = jnp.minimum(local // CAP, GROUPS - 1)
    moving = local < GROUPS * CAP
    target = jnp.where(moving, sigma[(inv_sigma[device] + shifts[group]) % owners], device)
    slot = jnp.broadcast_to(local, (owners, BLK_DEV))
    order = jax.vmap(lambda inner: jax.random.permutation(inner, BLK_DEV))(jax.random.split(keys[3], owners))
    place = target * BLK_DEV + order[target, slot]
    shuffle = jax.vmap(lambda inner: jax.random.permutation(inner, BLK_DEV))(jax.random.split(keys[4], owners))
    source = device * BLK_DEV + shuffle
    return jnp.zeros((BLOCKS,), jnp.int32).at[source.reshape(-1)].set(place.reshape(-1).astype(jnp.int32))


def draw_neighbours(key, part):
    key = jax.random.fold_in(key, 12)
    keys = jax.random.split(key, 3)
    position = jnp.arange(BLOCKS)[:, None, None]
    face = jnp.arange(4)[None, :, None]
    entry = jnp.arange(4)[None, None, :]
    kind = jax.random.randint(keys[0], (BLOCKS, 4, 1), 0, 10)
    sign = jax.random.randint(keys[1], (BLOCKS, 4, 4), 0, 2) * 2 - 1
    offset = jax.random.randint(keys[2], (BLOCKS, 4, 4), 1, REACH + 1) * sign
    forced = (position % BLK_DEV == BLK_DEV // 2) & (face == 1)
    offset = jnp.where(forced, REACH, offset)
    kind = jnp.where(forced, 1, kind)
    ahead = position + offset
    ahead = jnp.where((ahead < 0) | (ahead >= BLOCKS), position - offset, ahead)
    live = (kind >= 1) & ((kind >= 7) | (entry == 0))
    table = jnp.where(live, ahead, -1)
    table = table.at[0, 0].set(jnp.full((4,), -1, jnp.int32))
    table = table.at[BLOCKS - 2, 1].set(jnp.array([BLOCKS - 1, -1, -1, -1], jnp.int32))
    return table.astype(jnp.int32)


def with_ends(result, stream_key, smallest, top_value):
    longest = result.shape.index(max(result.shape))
    spots = []
    for shift in (0, 1):
        where = [jax.random.randint(jax.random.fold_in(stream_key, axis), (), 0, length) for axis, length in enumerate(result.shape)]
        where[longest] = (where[longest] + shift) % result.shape[longest]
        spots.append(tuple(where))
    return result.at[spots[0]].set(smallest).at[spots[1]].set(top_value)


def block_levels(key, shape, shards, low, high):
    loudness = 1.0
    for dim, shards_of in shards:
        steps = jax.random.uniform(jax.random.fold_in(jax.random.fold_in(key, 6), dim), (shards_of,), jnp.float32, low / len(shards), high / len(shards))
        loudness = loudness * jnp.repeat(jnp.exp(steps), shape[dim] // shards_of).reshape((-1,) + (1,) * (len(shape) - 1 - dim))
    return loudness


def setup_inputs(seed: int = 0) -> dict:
    arg_keys = jax.random.split(jax.random.key(seed), 11)
    head = jnp.clip(-1.5 + 1.8 * jax.random.uniform(arg_keys[0], (LAYERS, BLOCKS, CELLS), jnp.float32) ** block_levels(arg_keys[0], (LAYERS, BLOCKS, CELLS), ((0, 16), (1, 16)), -0.2, 0.2), -1.5, 0.3)
    water_prev = jnp.clip(0.05 + 0.35 * jax.random.uniform(arg_keys[1], (LAYERS, BLOCKS, CELLS), jnp.float32) ** block_levels(arg_keys[1], (LAYERS, BLOCKS, CELLS), ((0, 16), (1, 16)), -0.2, 0.2), 0.05, 0.4)
    alpha = jnp.clip(jnp.exp(math.log(3.0) - 2.3025851 * jax.random.uniform(arg_keys[2], (LAYERS, BLOCKS, CELLS), jnp.float32) ** block_levels(arg_keys[2], (LAYERS, BLOCKS, CELLS), ((0, 16), (1, 16)), -0.2, 0.2)), 0.3, 3.0)
    shape_n = jnp.clip(1.3 + 1.7 * jax.random.uniform(arg_keys[3], (LAYERS, BLOCKS, CELLS), jnp.float32) ** block_levels(arg_keys[3], (LAYERS, BLOCKS, CELLS), ((0, 16), (1, 16)), -0.2, 0.2), 1.3, 3.0)
    theta_r = jnp.clip(0.02 + 0.08 * jax.random.uniform(arg_keys[4], (LAYERS, BLOCKS, CELLS), jnp.float32) ** block_levels(arg_keys[4], (LAYERS, BLOCKS, CELLS), ((0, 16), (1, 16)), -0.2, 0.2), 0.02, 0.1)
    theta_s = jnp.clip(0.35 + 0.15 * jax.random.uniform(arg_keys[5], (LAYERS, BLOCKS, CELLS), jnp.float32) ** block_levels(arg_keys[5], (LAYERS, BLOCKS, CELLS), ((0, 16), (1, 16)), -0.2, 0.2), 0.35, 0.5)
    sat_cond = jnp.clip(jnp.exp(math.log(5.0) - 2.3025851 * jax.random.uniform(arg_keys[6], (LAYERS, BLOCKS, CELLS), jnp.float32) ** block_levels(arg_keys[6], (LAYERS, BLOCKS, CELLS), ((0, 16), (1, 16)), -0.2, 0.2)), 0.5, 5.0)
    refine = with_ends(jax.random.randint(arg_keys[7], (BLOCKS,), 0, 9), jax.random.fold_in(arg_keys[7], 1), 0, 8).astype(jnp.int32)
    destination = draw_destination(jax.random.fold_in(arg_keys[10], 71), 0)
    neighbours = draw_neighbours(jax.random.fold_in(arg_keys[10], 71), 0)
    return {"head": head, "water_prev": water_prev, "alpha": alpha, "shape_n": shape_n, "theta_r": theta_r, "theta_s": theta_s, "sat_cond": sat_cond, "refine": refine, "destination": destination, "neighbours": neighbours}


inv_step = 4.0

def line_tables(bit):
    low_index = []
    high_index = []
    low_weight = []
    high_weight = []
    for fine in range(8):
        half = fine // 2
        if fine % 2 == 0:
            low_index.append(max(4 * bit + half - 1, 0))
            high_index.append(4 * bit + half)
            low_weight.append(0.25)
            high_weight.append(0.75)
        else:
            low_index.append(4 * bit + half)
            high_index.append(min(4 * bit + half + 1, 7))
            low_weight.append(0.75)
            high_weight.append(0.25)
    return (np.array(low_index), np.array(high_index), np.array(low_weight, np.float32), np.array(high_weight, np.float32))

def along(cube, axis_pos, bits, smooth):
    shape = [1, 1, 1, 1, 1]
    shape[axis_pos] = 8
    results = []
    for bit in range(2):
        low_index, high_index, low_weight, high_weight = line_tables(bit)
        if smooth:
            value = jnp.take(cube, low_index, axis=axis_pos) * low_weight.reshape(shape) + jnp.take(cube, high_index, axis=axis_pos) * high_weight.reshape(shape)
        else:
            value = jnp.take(cube, np.array([4 * bit + fine // 2 for fine in range(8)]), axis=axis_pos)
        results.append(value)
    chosen = bits.reshape(1, -1, 1, 1, 1) == 1
    return jnp.where(chosen, results[1], results[0])

def adapt(fields, flags, smooth):
    octant = jnp.maximum(flags - 1, 0)
    cube = fields.reshape(fields.shape[0], fields.shape[1], 8, 8, 8)
    cube = along(cube, 2, octant // 4, smooth)
    cube = along(cube, 3, octant // 2 % 2, smooth)
    cube = along(cube, 4, octant % 2, smooth)
    return jnp.where((flags == 0).reshape(1, -1, 1), fields, cube.reshape(fields.shape))

def closure(head_cell, cell_alpha, cell_shape, cell_resid, cell_sat, cell_cond):
    expo = 1.0 - 1.0 / cell_shape
    ratio = jnp.power(cell_alpha * jnp.maximum(-head_cell, 0.0), cell_shape)
    saturation = jnp.power(1.0 + ratio, -expo)
    water = cell_resid + (cell_sat - cell_resid) * saturation
    inner = 1.0 - jnp.power(ratio / (1.0 + ratio), expo)
    conduct = cell_cond * jnp.sqrt(saturation) * inner * inner
    return (water, conduct)

def lateral_faces(cells):
    cube = cells.reshape(-1, 8, 8, 8)
    return jnp.stack([cube[:, 0], cube[:, 7], cube[:, :, 0], cube[:, :, 7]], axis=1).reshape(-1, 4, 64)

def quad_table():
    table = np.zeros((64, 4), np.int32)
    for first in range(8):
        for second in range(8):
            quarter = first // 4 * 2 + second // 4
            for pair in range(4):
                table[first * 8 + second, pair] = quarter * 64 + (2 * (first % 4) + pair // 2) * 8 + 2 * (second % 4) + pair % 2
    return table

def ghost_values(source, table_nb):
    blocks = table_nb.shape[0]
    safe = jnp.maximum(table_nb, 0)
    opposite = np.array([1, 0, 3, 2]).reshape(1, 4, 1)
    picked = source[safe, opposite]
    conform = picked[:, :, 0]
    spread = picked.transpose(0, 1, 3, 2, 4).reshape(blocks, 4, 2, 256)
    finer = jnp.take(spread, quad_table().reshape(-1), axis=3).reshape(blocks, 4, 2, 64, 4)
    hanging = 0.25 * (finer[..., 0] + finer[..., 1] + finer[..., 2] + finer[..., 3])
    count = lax.optimization_barrier(jnp.sum((table_nb >= 0).astype(jnp.int32), axis=2))
    value = jnp.where((count == 4)[:, :, None, None], hanging, conform)
    present = (count > 0).astype(jnp.float32)
    return (value, present)

def beside(cube, plane, axis_pos, first):
    plane = jnp.expand_dims(plane, axis_pos)
    if first:
        return jnp.concatenate([plane, lax.slice_in_dim(cube, 0, 7, axis=axis_pos)], axis=axis_pos)
    return jnp.concatenate([lax.slice_in_dim(cube, 1, 8, axis=axis_pos), plane], axis=axis_pos)

def balance(head_cell, water, conduct, prior, cell_alpha, cell_resid, cell_sat, lat_value, lat_on, below, above, low_on, high_on):
    blocks = head_cell.shape[0]
    cube_h = head_cell.reshape(blocks, 8, 8, 8)
    cube_k = conduct.reshape(blocks, 8, 8, 8)
    ones = jnp.ones_like(cube_h)
    flux = jnp.zeros_like(cube_h)
    total = jnp.zeros_like(cube_h)
    plans = []
    for face, axis_pos, first in ((0, 1, True), (1, 1, False), (2, 2, True), (3, 2, False)):
        plane_on = ones[:, 0] * lat_on[:, face].reshape(blocks, 1, 1)
        plans.append((lat_value[:, face, 0].reshape(blocks, 8, 8), lat_value[:, face, 1].reshape(blocks, 8, 8), plane_on, axis_pos, first, 0.0))
    plans.append((below[:, 0].reshape(blocks, 8, 8), below[:, 1].reshape(blocks, 8, 8), ones[:, 0] * low_on, 3, True, -1.0))
    plans.append((above[:, 0].reshape(blocks, 8, 8), above[:, 1].reshape(blocks, 8, 8), ones[:, 0] * high_on, 3, False, 1.0))
    for plane_h, plane_k, plane_on, axis_pos, first, lift in plans:
        near_h = beside(cube_h, plane_h, axis_pos, first)
        near_k = beside(cube_k, plane_k, axis_pos, first)
        near_on = beside(ones, plane_on, axis_pos, first)
        face_k = near_on * 0.5 * (cube_k + near_k)
        flux = flux + face_k * (near_h - cube_h + lift)
        total = total + face_k
    resid = inv_step * (water - prior) - flux.reshape(blocks, -1)
    diagonal = inv_step * (cell_sat - cell_resid) * cell_alpha + total.reshape(blocks, -1)
    return (resid, diagonal)

def planes(cells, conduct, level_k):
    layers, blocks = (cells.shape[0], cells.shape[1])
    plane_h = cells.reshape(layers, blocks, 8, 8, 8)[..., level_k].reshape(layers, blocks, 64)
    plane_k = conduct.reshape(layers, blocks, 8, 8, 8)[..., level_k].reshape(layers, blocks, 64)
    return jnp.stack([plane_h, plane_k], axis=2)

def evaluate(head_all, prior, cell_alpha, cell_shape, cell_resid, cell_sat, cell_cond, neighbours):
    water, conduct = closure(head_all, cell_alpha, cell_shape, cell_resid, cell_sat, cell_cond)
    layers = head_all.shape[0]
    bottoms = planes(head_all, conduct, 0)
    tops = planes(head_all, conduct, 7)
    empty = jnp.zeros_like(tops[:1])
    below = jnp.concatenate([empty, tops[:-1]], axis=0)
    above = jnp.concatenate([bottoms[1:], empty], axis=0)
    level = jnp.arange(layers)
    low_on = (level > 0).astype(jnp.float32)
    high_on = (level < layers - 1).astype(jnp.float32)

    def one_layer(items):
        head_l, water_l, cond_l, prior_l, alpha_l, resid_l, sat_l, below_l, above_l, low_l, high_l = items
        faces = jnp.stack([lateral_faces(head_l), lateral_faces(cond_l)], axis=2)
        lat_value, lat_on = ghost_values(faces, neighbours)
        return balance(head_l, water_l, cond_l, prior_l, alpha_l, resid_l, sat_l, lat_value, lat_on, below_l, above_l, low_l, high_l)
    return lax.map(one_layer, (head_all, water, conduct, prior, cell_alpha, cell_resid, cell_sat, below, above, low_on, high_on))

def reference(head, water_prev, alpha, shape_n, theta_r, theta_s, sat_cond, refine, destination, neighbours):
    adapted = [adapt(field, refine, True) for field in (head, water_prev)]
    adapted = adapted + [adapt(field, refine, False) for field in (alpha, shape_n, theta_r, theta_s, sat_cond)]
    moved = [jnp.zeros_like(field).at[:, destination].set(field) for field in adapted]
    start, prior, cell_alpha, cell_shape, cell_resid, cell_sat, cell_cond = moved
    resid, diagonal = evaluate(start, prior, cell_alpha, cell_shape, cell_resid, cell_sat, cell_cond, neighbours)
    new_head = start - resid / diagonal
    final, unused = evaluate(new_head, prior, cell_alpha, cell_shape, cell_resid, cell_sat, cell_cond, neighbours)
    return (new_head, final)
```

```python
import jax
import jax.numpy as jnp
from jax import lax
from jax.experimental import pallas as pl
from jax.experimental.pallas import tpu as pltpu
from jax.sharding import PartitionSpec as P

peers = 16
blocks = 64
fields = 6
room = 4
reach = 16
rows = fields * 4
chunk = room * rows + 8
vmem = 48 * 1024 * 1024
f32 = jnp.float32


def lane_take(x, index):
    numbers = lax.GatherDimensionNumbers((), (1,), (1,), (0,), (0,))
    return lax.gather(x, index[..., None], numbers, (1, 1), mode=lax.GatherScatterMode.PROMISE_IN_BOUNDS)


def row_take(x, index):
    numbers = lax.GatherDimensionNumbers((), (0,), (0,), (1,), (1,))
    return lax.gather(x, index[..., None], numbers, (1, 1), mode=lax.GatherScatterMode.PROMISE_IN_BOUNDS)


def iota(shape, axis):
    return lax.broadcasted_iota(jnp.int32, shape, axis)


def turn(x, shift, axis=None):
    axis = x.ndim - 1 if axis is None else axis
    shift = shift % x.shape[axis]
    if shift == 0:
        return x
    if x.ndim == 2:
        return pltpu.roll(x, shift, axis)
    flat = pltpu.roll(x.reshape(-1, x.shape[-1]), shift, 1)
    return flat.reshape(x.shape)


def pack_kernel(*refs):
    sources, (send, own, stay), (work, flags, count) = refs[:9], refs[9:12], refs[12:15]
    held, sems = refs[15:24], refs[24]
    copies = [pltpu.make_async_copy(source, ref, sems.at[n]) for n, (source, ref) in enumerate(zip(sources, held))]
    for copy in copies:
        copy.start()
    refine, destination, head, prior, alpha, shape_n, resid, sat, cond = held
    me = lax.axis_index("dom")
    for copy in copies:
        copy.wait()
    for peer in range(peers):
        count[peer] = 0
    for block in range(blocks):
        flags[pl.ds(block, 1), :] = jnp.full((1, 128), refine[block], jnp.int32)
    lane = iota((blocks, 128), 1)
    half, fine_y, fine_z = (lane >> 6) & 1, (lane >> 3) & 7, lane & 7
    flag = flags[...]
    octant = jnp.maximum(flag - 1, 0)
    kept = flag == 0
    bit_x, bit_y, bit_z = (octant >> 2) & 1, (octant >> 1) & 1, octant & 1
    up_x = bit_x == 1

    def get(ref):
        return [ref[0, :, 128 * c : 128 * c + 128] for c in range(4)]

    plain_y, plain_z = 4 * bit_y + (fine_y >> 1), 4 * bit_z + (fine_z >> 1)
    inner = plain_y * 8 + plain_z
    plain_index = [jnp.where(kept, lane, parity * 64 + inner) for parity in range(2)]

    def plain(v):
        chosen = [
            jnp.where(up_x, v[2], v[0]),
            jnp.where(kept, v[1], jnp.where(up_x, v[2], v[0])),
            jnp.where(kept, v[2], jnp.where(up_x, v[3], v[1])),
            jnp.where(kept | up_x, v[3], v[1]),
        ]
        return [lane_take(chosen[c], plain_index[c % 2]) for c in range(4)]

    side_y = jnp.clip(plain_y + 2 * (fine_y & 1) - 1, 0, 7)
    side_z = jnp.clip(plain_z + 2 * (fine_z & 1) - 1, 0, 7)
    near_y = half * 64 + plain_y * 8 + fine_z
    far_y = half * 64 + side_y * 8 + fine_z
    near_z = (lane & 120) + plain_z
    far_z = (lane & 120) + side_z
    lower = lane < 64

    def smooth(v):
        r = [turn(x, 64) for x in v]
        base = [jnp.where(up_x, v[2 + c], v[c]) for c in range(2)]
        base_r = [jnp.where(up_x, r[2 + c], r[c]) for c in range(2)]
        near = [
            jnp.where(lower, base[0], base_r[0]),
            jnp.where(lower, base_r[0], base[0]),
            jnp.where(lower, base[1], base_r[1]),
            jnp.where(lower, base_r[1], base[1]),
        ]
        far = [
            jnp.where(lower, jnp.where(up_x, r[1], v[0]), base[0]),
            jnp.where(lower, base[0], jnp.where(up_x, r[3], r[1])),
            jnp.where(lower, base_r[0], base[1]),
            jnp.where(lower, base[1], jnp.where(up_x, v[3], r[2])),
        ]
        result = []
        for c in range(4):
            x = 0.75 * near[c] + 0.25 * far[c]
            x = 0.75 * lane_take(x, near_y) + 0.25 * lane_take(x, far_y)
            x = 0.75 * lane_take(x, near_z) + 0.25 * lane_take(x, far_z)
            result.append(jnp.where(kept, v[c], x))
        return result

    low = get(resid)
    span = [high - bottom for high, bottom in zip(get(sat), low)]
    moved = [
        smooth(get(head)),
        [a - b for a, b in zip(plain(low), smooth(get(prior)))],
        plain(get(alpha)),
        plain(get(shape_n)),
        plain(get(cond)),
        plain(span),
    ]
    for f in range(fields):
        for c in range(4):
            own[pl.ds((f * 4 + c) * blocks, blocks), :] = moved[f][c]
            for g in range(blocks // 8):
                part = moved[f][c][8 * g : 8 * g + 8]
                work[pl.ds(8 * g * rows + f * 4 + c, 8, stride=rows), :] = part

    for peer in range(peers):
        send[pl.ds(peer * chunk + room * rows, 8), :] = jnp.full((8, 128), -1.0, f32)

    for block in range(blocks):
        target = destination[block]
        owner = target >> 6
        used = count[owner] & (room - 1)
        count[owner] = used + 1
        spot = jnp.full((1, 128), target & 63, jnp.int32).astype(f32)
        start = pl.multiple_of(owner * chunk + used * rows, 8)
        send[pl.ds(start, rows), :] = work[block * rows : block * rows + rows, :]
        send[pl.ds(owner * chunk + room * rows + used, 1), :] = spot
        stay[block : block + 1, :] = jnp.where(owner == me, spot, -1.0)
    send[pl.ds(pl.multiple_of(me * chunk + room * rows, 8), 8), :] = jnp.full((8, 128), -1.0, f32)


def find(places):
    hit = places == (iota((blocks, 128), 1) & 63).astype(f32)
    row = jnp.sum(jnp.where(hit, iota((blocks, 128), 0), 0), axis=0, keepdims=True)
    has = jnp.sum(jnp.where(hit, 1, 0), axis=0, keepdims=True) > 0
    return row + (iota((1, 128), 1) & 64), has


def settle_kernel(own, stay, out):
    index, _ = find(stay[...])
    index = jnp.broadcast_to(index, (128, 128))
    for f in range(fields):
        for c in range(2):
            lo = own[(f * 4 + c) * blocks : (f * 4 + c + 1) * blocks, :]
            hi = own[(f * 4 + c + 2) * blocks : (f * 4 + c + 3) * blocks, :]
            cells = jnp.concatenate([lo, hi], axis=0).T
            out[f, 128 * c : 128 * c + 128, :] = lane_take(cells, index)


def closure(head, less, alpha, shape_n, cond, span):
    expo = 1.0 - 1.0 / shape_n
    log_t = shape_n * jnp.log(alpha * jnp.maximum(-head, 0.0))
    log_s = jnp.log(1.0 + jnp.exp(log_t))
    root = jnp.exp(-0.5 * expo * log_s)
    inner = 1.0 - jnp.exp(expo * (log_t - log_s))
    return cond * root * inner * inner, 4.0 * (less + span * root * root)


def cube(x):
    return x.reshape(4, 8, 8, 128)


def face_tiles(x):
    y0, y7 = x[:, 0], x[:, 7]
    return [
        x[0],
        turn(x[3], 64),
        jnp.concatenate([y0, turn(y0, 64)], axis=0),
        jnp.concatenate([y7, turn(y7, 64)], axis=0),
    ]


def pack_faces(tiles_h, tiles_k, first):
    group = iota((8, 8, 128), 2) >> 4
    packed = None
    for f in range(4):
        for q, tiles in enumerate((tiles_h, tiles_k)):
            part = turn(tiles[f], (2 * f + q) * reach - first)
            packed = part if packed is None else jnp.where(group == 2 * f + q, part, packed)
    return packed.reshape(64, 128)


def emit(head_ref, cond_ref, right, left, up, down):
    tiles_h, tiles_k = face_tiles(cube(head_ref[...])), face_tiles(cube(cond_ref[...]))
    right[...] = pack_faces(tiles_h, tiles_k, blocks - reach)
    left[...] = pack_faces(tiles_h, tiles_k, 0)
    for q, ref in enumerate((head_ref, cond_ref)):
        up[32 * q : 32 * q + 32, :] = ref[pl.ds(7, 32, stride=8), :]
        down[32 * q : 32 * q + 32, :] = ref[pl.ds(0, 32, stride=8), :]


def arrive_kernel(recv, settled, state, cond_out, water_out, right, left, up, down):
    def slots(start):
        return [recv[pl.ds(start(o), peers, stride=chunk), :] for o in range(room)]

    places = jnp.concatenate(slots(lambda o: room * rows + o), axis=0)
    index, has = find(places)
    index = jnp.broadcast_to(index, (128, 128))
    for f in range(fields):
        for c in range(2):
            parts = slots(lambda o: o * rows + f * 4 + c) + slots(lambda o: o * rows + f * 4 + c + 2)
            cells = jnp.concatenate(parts, axis=0).T
            span = slice(128 * c, 128 * c + 128)
            state[f, span, :] = jnp.where(has, lane_take(cells, index), settled[f, span, :])
    cond, water = closure(*[state[f] for f in range(fields)])
    cond_out[...] = cond
    water_out[...] = water
    emit(state.at[0], cond_out, right, left, up, down)


class Table:
    def __init__(self, near):
        position = near[...] - lax.axis_index("dom") * blocks
        spot = jnp.where(position < 0, position + 80, jnp.where(position >= blocks, position + reach, position))
        present = near[...] >= 0
        spot = jnp.where(present, spot, 0)
        lower = iota((8, 128), 1) < 64
        front = iota((8, 128), 0) < 4

        def row(f, e):
            return jnp.broadcast_to(spot[4 * f + e : 4 * f + e + 1], (8, 128))

        def on(f, e):
            return jnp.broadcast_to(present[4 * f + e : 4 * f + e + 1].astype(jnp.int32), (8, 128)) == 1

        self.lower = lower
        self.one_x = jnp.where(lower, row(0, 0), row(1, 0))
        self.four_x = [
            jnp.where(
                lower,
                jnp.where(front, row(0, 2 * s), row(0, 2 * s + 1)),
                jnp.where(front, row(1, 2 * s), row(1, 2 * s + 1)),
            )
            for s in range(2)
        ]
        self.hang_x = (lower & on(0, 3)) | (~lower & on(1, 3))
        self.on_x = (lower & on(0, 0)) | (~lower & on(1, 0))
        self.one_y = [row(f, 0) for f in (2, 3)]
        self.four_y = [
            jnp.where(
                lower,
                jnp.where(front, row(f, 0), row(f, 1)),
                jnp.where(front, row(f, 2), row(f, 3)),
            )
            for f in (2, 3)
        ]
        self.hang_y = [on(f, 3) for f in (2, 3)]
        self.on_y = [on(f, 0) for f in (2, 3)]


def quarters(tile):
    pick = (iota((8, 128), 0) & 3) * 2
    result = []
    for a in range(4):
        pair = tile[2 * a] + tile[2 * a + 1]
        pair = 0.25 * (pair + turn(pair, 7, 0))
        result.append(row_take(pair, pick))
    return result


def ghosts(x, left, right, q, table):
    lane = iota((8, 8, 128), 2)
    tiles = []
    for f, tile in enumerate(face_tiles(x)):
        g = 2 * f + q
        after = jnp.where(lane < 80, turn(left, 64 - g * reach), turn(right, 80 - g * reach))
        tiles.append(jnp.where(lane < 64, tile, after))
    coarse = [quarters(tile) for tile in tiles]
    low = table.lower
    face_x = []
    for a in range(8):
        one = jnp.where(low, lane_take(tiles[1][a], table.one_x), lane_take(tiles[0][a], table.one_x))
        index = table.four_x[a // 4]
        four = jnp.where(low, lane_take(coarse[1][a % 4], index), lane_take(coarse[0][a % 4], index))
        face_x.append(jnp.where(table.hang_x, four, one))
    face_y = []
    for side, source in ((0, 3), (1, 2)):
        made = []
        for a in range(4):
            index = table.one_y[side]
            one = jnp.where(low, lane_take(tiles[source][a], index), lane_take(tiles[source][a + 4], index))
            four = lane_take(coarse[source][a], table.four_y[side])
            made.append(jnp.where(table.hang_y[side], four, one))
        face_y.append(jnp.stack(made))
    return jnp.stack(face_x), face_y[0], face_y[1]


def balance(head, cond, left, right, below, above, near, planes):
    table = Table(near)
    level = lax.axis_index("depth")
    left, right = left[...].reshape(8, 8, 128), right[...].reshape(8, 8, 128)
    ghost_h = ghosts(head, left, right, 0, table)
    ghost_k = ghosts(cond, left, right, 1, table)
    for q in range(2):
        planes[2 * q, pl.ds(0, 32, stride=8), :] = below[32 * q : 32 * q + 32, :]
        planes[2 * q + 1, pl.ds(7, 32, stride=8), :] = above[32 * q : 32 * q + 32, :]
    level_k = iota((4, 8, 8, 128), 2)
    low = iota((8, 8, 128), 2) < 64

    def neighbours(x, ghost, q):
        around, y2, y3 = ghost
        x0, x3 = turn(x[0], 64), turn(x[3], 64)
        return [
            jnp.concatenate([jnp.where(low, around, x3)[None], x[:3]], axis=0),
            jnp.concatenate([x[1:], jnp.where(low, x0, around)[None]], axis=0),
            jnp.concatenate([y2[:, None], x[:, :7]], axis=1),
            jnp.concatenate([x[:, 1:], y3[:, None]], axis=1),
            jnp.where(level_k == 0, cube(planes[2 * q]), cube(turn(x.reshape(256, 128), 1, 0))),
            jnp.where(level_k == 7, cube(planes[2 * q + 1]), cube(turn(x.reshape(256, 128), 255, 0))),
        ]

    slab = iota((4, 8, 8, 128), 0)
    row_j = iota((4, 8, 8, 128), 1)
    lower = iota((4, 8, 8, 128), 3) < 64
    off_x, off_y = ~table.on_x, [~on for on in table.on_y]
    closed = [
        (slab == 0) & lower & off_x,
        (slab == 3) & ~lower & off_x,
        (row_j == 0) & off_y[0],
        (row_j == 7) & off_y[1],
        (level_k == 0) & (level == 0),
        (level_k == 7) & (level == lax.axis_size("depth") - 1),
    ]
    flux = total = None
    pairs = zip(neighbours(head, ghost_h, 0), neighbours(cond, ghost_k, 1), closed)
    for direction, (near_h, near_k, shut) in enumerate(pairs):
        face_k = jnp.where(shut, 0.0, cond + near_k)
        lift = (0.0, 0.0, 0.0, 0.0, -1.0, 1.0)[direction]
        part = jnp.where(shut, 0.0, face_k * (near_h - head + lift))
        flux = part if flux is None else flux + part
        total = face_k if total is None else total + face_k
    return 0.5 * flux, 0.5 * total


def newton_kernel(
    state, cond, water, left, right, below, above, near, head_out, cond_out, water_out, to_right, to_left, up, down, planes
):
    head = cube(state[0])
    flux, total = balance(head, cube(cond[...]), left, right, below, above, near, planes)
    resid = cube(water[...]) - flux
    diagonal = 4.0 * cube(state[5]) * cube(state[2]) + total
    head_out[...] = (head - resid / diagonal).reshape(256, 128)
    new_cond, new_water = closure(head_out[...], *[state[f] for f in range(1, fields)])
    cond_out[...] = new_cond
    water_out[...] = new_water
    emit(head_out, cond_out, to_right, to_left, up, down)


def leave(ref, cells):
    for c in range(2):
        turned = cells[128 * c : 128 * c + 128].T
        ref[0, :, 128 * c : 128 * c + 128] = turned[:blocks]
        ref[0, :, 128 * c + 256 : 128 * c + 384] = turned[blocks:]


def residual_kernel(head, cond, water, left, right, below, above, near, head_out, resid_out, planes):
    flux, _ = balance(cube(head[...]), cube(cond[...]), left, right, below, above, near, planes)
    leave(resid_out, water[...] - flux.reshape(256, 128))
    leave(head_out, head[...])


def shape(*dims):
    return jax.ShapeDtypeStruct(dims, f32)


def call(kernel, outs, scratch, *operands, source=pltpu.VMEM, limit=vmem):
    whole = pl.BlockSpec(memory_space=pltpu.VMEM)
    return pl.pallas_call(
        kernel,
        out_shape=outs,
        in_specs=[pl.BlockSpec(memory_space=source)] * len(operands),
        out_specs=[whole] * len(outs),
        scratch_shapes=scratch,
        compiler_params=pltpu.CompilerParams(vmem_limit_bytes=limit),
    )(*operands)


def exchange(to_right, to_left, up, down):
    def shifted(x, axis, step):
        size = lax.axis_size(axis)
        return lax.ppermute(x, axis, [(i, (i + step) % size) for i in range(size)])

    return (
        shifted(to_right, "dom", 1),
        shifted(to_left, "dom", -1),
        shifted(up, "depth", 1),
        shifted(down, "depth", -1),
    )


def on_device(head, water_prev, alpha, shape_n, theta_r, theta_s, sat_cond, refine, destination, neighbours):
    send, own, stay = call(
        pack_kernel,
        [shape(peers * chunk, 128), shape(rows * blocks, 128), shape(blocks, 128)],
        [pltpu.VMEM((blocks * rows, 128), f32), pltpu.VMEM((blocks, 128), jnp.int32), pltpu.SMEM((peers,), jnp.int32)]
        + [pltpu.SMEM((blocks,), jnp.int32)] * 2
        + [pltpu.VMEM((1, blocks, 512), f32)] * 7
        + [pltpu.SemaphoreType.DMA((9,))],
        refine, destination, head, water_prev, alpha, shape_n, theta_r, theta_s, sat_cond,
        source=pltpu.HBM,
        limit=64 * 1024 * 1024,
    )
    recv = lax.all_to_all(send.reshape(peers, chunk, 128), "dom", 0, 0, tiled=True)
    (settled,) = call(settle_kernel, [shape(fields, 256, 128)], [], own, stay)
    near = neighbours.reshape(blocks, 16).T
    near = jnp.concatenate([near, near], axis=1)
    cells, halo = shape(256, 128), [shape(64, 128)] * 4
    state, cond, water, *outgoing = call(
        arrive_kernel,
        [shape(fields, 256, 128), cells, cells] + halo,
        [],
        recv.reshape(peers * chunk, 128), settled,
    )
    planes = [pltpu.VMEM((4, 256, 128), f32)]
    new_head, cond, water, *outgoing = call(
        newton_kernel, [cells] * 3 + halo, planes, state, cond, water, *exchange(*outgoing), near
    )
    final = shape(1, blocks, 512)
    return tuple(
        call(residual_kernel, [final, final], planes, new_head, cond, water, *exchange(*outgoing), near)
    )


def solution(mesh):
    cells = P("depth", "dom", None)
    return jax.shard_map(
        on_device,
        mesh=mesh,
        in_specs=(cells,) * 7 + (P("dom"), P("dom"), P("dom", None, None)),
        out_specs=(cells, cells),
        check_vma=False,
    )
```

```python
import jax
import jax.numpy as jnp
from jax import lax
from jax.experimental import pallas as pl
from jax.experimental.pallas import tpu as pltpu
from jax.sharding import PartitionSpec as P

peers = 16
blocks = 64
fields = 6
room = 4
reach = 16
rows = fields * 4
late, early = 16, 8
chunk = room * rows + 8
vmem = 48 * 1024 * 1024
f32 = jnp.float32


def lane_take(x, index):
    numbers = lax.GatherDimensionNumbers((), (1,), (1,), (0,), (0,))
    return lax.gather(x, index[..., None], numbers, (1, 1), mode=lax.GatherScatterMode.PROMISE_IN_BOUNDS)


def row_take(x, index):
    numbers = lax.GatherDimensionNumbers((), (0,), (0,), (1,), (1,))
    return lax.gather(x, index[..., None], numbers, (1, 1), mode=lax.GatherScatterMode.PROMISE_IN_BOUNDS)


def iota(shape, axis):
    return lax.broadcasted_iota(jnp.int32, shape, axis)


def turn(x, shift, axis=None):
    axis = x.ndim - 1 if axis is None else axis
    shift = shift % x.shape[axis]
    if shift == 0:
        return x
    if x.ndim == 2:
        return pltpu.roll(x, shift, axis)
    flat = pltpu.roll(x.reshape(-1, x.shape[-1]), shift, 1)
    return flat.reshape(x.shape)


def pack_kernel(*refs):
    sources, targets, refs = refs[:9], refs[9:12], refs[12:]
    held, (own, send, stay), refs = refs[:9], refs[9:12], refs[12:]
    work_late, work_early, flags, count, slot_early, sems_in, sems_out = refs
    arriving = [pltpu.make_async_copy(source, ref, sems_in.at[n]) for n, (source, ref) in enumerate(zip(sources, held))]
    for copy in arriving:
        copy.start()
    leaving = []

    def depart(source, target):
        copy = pltpu.make_async_copy(source, target, sems_out.at[len(leaving)])
        copy.start()
        leaving.append(copy)

    refine, destination = held[:2]
    me = lax.axis_index("dom")
    for peer in range(peers):
        count[peer] = 0
    arriving[0].wait()
    for block in range(blocks):
        flags[pl.ds(block, 1), :] = jnp.full((1, 128), refine[block], jnp.int32)
    lane = iota((blocks, 128), 1)
    half, fine_y, fine_z = (lane >> 6) & 1, (lane >> 3) & 7, lane & 7
    flag = flags[...]
    octant = jnp.maximum(flag - 1, 0)
    kept = flag == 0
    bit_x, bit_y, bit_z = (octant >> 2) & 1, (octant >> 1) & 1, octant & 1
    up_x = bit_x == 1

    def get(n):
        arriving[n].wait()
        return [held[n][0, :, 128 * c : 128 * c + 128] for c in range(4)]

    plain_y, plain_z = 4 * bit_y + (fine_y >> 1), 4 * bit_z + (fine_z >> 1)
    inner = plain_y * 8 + plain_z
    plain_index = [jnp.where(kept, lane, parity * 64 + inner) for parity in range(2)]

    def plain(v):
        chosen = [
            jnp.where(up_x, v[2], v[0]),
            jnp.where(kept, v[1], jnp.where(up_x, v[2], v[0])),
            jnp.where(kept, v[2], jnp.where(up_x, v[3], v[1])),
            jnp.where(kept | up_x, v[3], v[1]),
        ]
        return [lane_take(chosen[c], plain_index[c % 2]) for c in range(4)]

    side_y = jnp.clip(plain_y + 2 * (fine_y & 1) - 1, 0, 7)
    side_z = jnp.clip(plain_z + 2 * (fine_z & 1) - 1, 0, 7)
    near_y = half * 64 + plain_y * 8 + fine_z
    far_y = half * 64 + side_y * 8 + fine_z
    near_z = (lane & 120) + plain_z
    far_z = (lane & 120) + side_z
    lower = lane < 64

    def smooth(v):
        r = [turn(x, 64) for x in v]
        base = [jnp.where(up_x, v[2 + c], v[c]) for c in range(2)]
        base_r = [jnp.where(up_x, r[2 + c], r[c]) for c in range(2)]
        near = [
            jnp.where(lower, base[0], base_r[0]),
            jnp.where(lower, base_r[0], base[0]),
            jnp.where(lower, base[1], base_r[1]),
            jnp.where(lower, base_r[1], base[1]),
        ]
        far = [
            jnp.where(lower, jnp.where(up_x, r[1], v[0]), base[0]),
            jnp.where(lower, base[0], jnp.where(up_x, r[3], r[1])),
            jnp.where(lower, base_r[0], base[1]),
            jnp.where(lower, base[1], jnp.where(up_x, v[3], r[2])),
        ]
        result = []
        for c in range(4):
            x = 0.75 * near[c] + 0.25 * far[c]
            x = 0.75 * lane_take(x, near_y) + 0.25 * lane_take(x, far_y)
            x = 0.75 * lane_take(x, near_z) + 0.25 * lane_take(x, far_z)
            result.append(jnp.where(kept, v[c], x))
        return result

    def keep(f, values, work, size, first):
        for c in range(4):
            own[f * 4 + c] = values[c]
            for g in range(blocks // 8):
                work[pl.ds(8 * g * size + (f - first) * 4 + c, 8, stride=size), :] = values[c][8 * g : 8 * g + 8]
        depart(own.at[4 * f : 4 * f + 4], targets[0].at[4 * f : 4 * f + 4])

    for n, f in ((2, 2), (3, 3), (4, 4)):
        keep(f, plain(get(n)), work_late, late, 2)
    high, low = get(5), get(6)
    keep(5, plain([x - y for x, y in zip(high, low)]), work_late, late, 2)

    arriving[1].wait()
    for peer in range(peers):
        send[peer, rows * room :, :] = jnp.full((8, 128), -1.0, f32)
    for block in range(blocks):
        target = destination[block]
        owner = target >> 6
        used = count[owner] & (room - 1)
        count[owner] = used + 1
        spot = jnp.full((1, 128), target & 63, jnp.int32).astype(f32)
        slot_early[block] = room * late + used * early
        start = pl.ds(pl.multiple_of(used * late, 8), late)
        send[owner, start, :] = work_late[block * late : block * late + late, :]
        send[owner, pl.ds(room * rows + used, 1), :] = spot
        stay[block : block + 1, :] = jnp.where(owner == me, spot, -1.0)
    send[me, rows * room :, :] = jnp.full((8, 128), -1.0, f32)
    depart(send.at[:, : room * late], targets[1].at[:, : room * late])
    depart(stay, targets[2])

    keep(0, smooth(get(7)), work_early, early, 0)
    keep(1, [x - y for x, y in zip(plain(low), smooth(get(8)))], work_early, early, 0)
    for block in range(blocks):
        start = pl.ds(pl.multiple_of(slot_early[block], 8), early)
        send[destination[block] >> 6, start, :] = work_early[block * early : block * early + early, :]
    depart(send.at[:, room * late :], targets[1].at[:, room * late :])
    for copy in leaving:
        copy.wait()


def find(places):
    hit = places == (iota((blocks, 128), 1) & 63).astype(f32)
    row = jnp.sum(jnp.where(hit, iota((blocks, 128), 0), 0), axis=0, keepdims=True)
    has = jnp.sum(jnp.where(hit, 1, 0), axis=0, keepdims=True) > 0
    return row + (iota((1, 128), 1) & 64), has


def settle_kernel(own, stay, out):
    index, _ = find(stay[...])
    index = jnp.broadcast_to(index, (128, 128))
    for f in range(fields):
        for c in range(2):
            cells = jnp.concatenate([own[f * 4 + c], own[f * 4 + c + 2]], axis=0).T
            out[f, 128 * c : 128 * c + 128, :] = lane_take(cells, index)


def closure(head, less, alpha, shape_n, cond, span):
    expo = 1.0 - 1.0 / shape_n
    log_t = shape_n * jnp.log(alpha * jnp.maximum(-head, 0.0))
    log_s = jnp.log(1.0 + jnp.exp(log_t))
    root = jnp.exp(-0.5 * expo * log_s)
    inner = 1.0 - jnp.exp(expo * (log_t - log_s))
    return cond * root * inner * inner, 4.0 * (less + span * root * root)


def cube(x):
    return x.reshape(4, 8, 8, 128)


def face_tiles(x):
    y0, y7 = x[:, 0], x[:, 7]
    return [
        x[0],
        turn(x[3], 64),
        jnp.concatenate([y0, turn(y0, 64)], axis=0),
        jnp.concatenate([y7, turn(y7, 64)], axis=0),
    ]


def pack_faces(tiles_h, tiles_k, first):
    group = iota((8, 8, 128), 2) >> 4
    packed = None
    for f in range(4):
        for q, tiles in enumerate((tiles_h, tiles_k)):
            part = turn(tiles[f], (2 * f + q) * reach - first)
            packed = part if packed is None else jnp.where(group == 2 * f + q, part, packed)
    return packed.reshape(64, 128)


def even(axis):
    return lax.axis_index(axis) % 2 == 0


def emit(head_ref, cond_ref, near, far, core, chip):
    tiles_h, tiles_k = face_tiles(cube(head_ref[...])), face_tiles(cube(cond_ref[...]))
    right = pack_faces(tiles_h, tiles_k, blocks - reach)
    left = pack_faces(tiles_h, tiles_k, 0)
    near[...] = jnp.where(even("dom"), right, left)
    far[...] = jnp.where(even("dom"), left, right)
    for q, ref in enumerate((head_ref, cond_ref)):
        top, bottom = ref[pl.ds(7, 32, stride=8), :], ref[pl.ds(0, 32, stride=8), :]
        core[32 * q : 32 * q + 32, :] = jnp.where(even("depth"), top, bottom)
        chip[32 * q : 32 * q + 32, :] = jnp.where(even("depth"), bottom, top)


def arrive_kernel(recv, settled, state, cond_out, water_out, *outgoing):
    def slots(start):
        return [recv[pl.ds(start(o), peers, stride=chunk), :] for o in range(room)]

    places = jnp.concatenate(slots(lambda o: room * rows + o), axis=0)
    index, has = find(places)
    index = jnp.broadcast_to(index, (128, 128))
    for f in range(fields):
        for c in range(2):
            parts = []
            for r in (c, c + 2):
                if f < 2:
                    parts += slots(lambda o: room * late + o * early + f * 4 + r)
                else:
                    parts += slots(lambda o: o * late + (f - 2) * 4 + r)
            cells = jnp.concatenate(parts, axis=0).T
            span = slice(128 * c, 128 * c + 128)
            state[f, span, :] = jnp.where(has, lane_take(cells, index), settled[f, span, :])
    cond, water = closure(*[state[f] for f in range(fields)])
    cond_out[...] = cond
    water_out[...] = water
    emit(state.at[0], cond_out, *outgoing)


class Table:
    def __init__(self, near):
        position = near[...] - lax.axis_index("dom") * blocks
        spot = jnp.where(position < 0, position + 80, jnp.where(position >= blocks, position + reach, position))
        present = near[...] >= 0
        spot = jnp.where(present, spot, 0)
        lower = iota((8, 128), 1) < 64
        front = iota((8, 128), 0) < 4

        def row(f, e):
            return jnp.broadcast_to(spot[4 * f + e : 4 * f + e + 1], (8, 128))

        def on(f, e):
            return jnp.broadcast_to(present[4 * f + e : 4 * f + e + 1].astype(jnp.int32), (8, 128)) == 1

        self.lower = lower
        self.one_x = jnp.where(lower, row(0, 0), row(1, 0))
        self.four_x = [
            jnp.where(
                lower,
                jnp.where(front, row(0, 2 * s), row(0, 2 * s + 1)),
                jnp.where(front, row(1, 2 * s), row(1, 2 * s + 1)),
            )
            for s in range(2)
        ]
        self.hang_x = (lower & on(0, 3)) | (~lower & on(1, 3))
        self.on_x = (lower & on(0, 0)) | (~lower & on(1, 0))
        self.one_y = [row(f, 0) for f in (2, 3)]
        self.four_y = [
            jnp.where(
                lower,
                jnp.where(front, row(f, 0), row(f, 1)),
                jnp.where(front, row(f, 2), row(f, 3)),
            )
            for f in (2, 3)
        ]
        self.hang_y = [on(f, 3) for f in (2, 3)]
        self.on_y = [on(f, 0) for f in (2, 3)]


def quarters(tile):
    pick = (iota((8, 128), 0) & 3) * 2
    result = []
    for a in range(4):
        pair = tile[2 * a] + tile[2 * a + 1]
        pair = 0.25 * (pair + turn(pair, 7, 0))
        result.append(row_take(pair, pick))
    return result


def ghosts(x, left, right, q, table):
    lane = iota((8, 8, 128), 2)
    tiles = []
    for f, tile in enumerate(face_tiles(x)):
        g = 2 * f + q
        after = jnp.where(lane < 80, turn(left, 64 - g * reach), turn(right, 80 - g * reach))
        tiles.append(jnp.where(lane < 64, tile, after))
    coarse = [quarters(tile) for tile in tiles]
    low = table.lower
    face_x = []
    for a in range(8):
        one = jnp.where(low, lane_take(tiles[1][a], table.one_x), lane_take(tiles[0][a], table.one_x))
        index = table.four_x[a // 4]
        four = jnp.where(low, lane_take(coarse[1][a % 4], index), lane_take(coarse[0][a % 4], index))
        face_x.append(jnp.where(table.hang_x, four, one))
    face_y = []
    for side, source in ((0, 3), (1, 2)):
        made = []
        for a in range(4):
            index = table.one_y[side]
            one = jnp.where(low, lane_take(tiles[source][a], index), lane_take(tiles[source][a + 4], index))
            four = lane_take(coarse[source][a], table.four_y[side])
            made.append(jnp.where(table.hang_y[side], four, one))
        face_y.append(jnp.stack(made))
    return jnp.stack(face_x), face_y[0], face_y[1]


def balance(head, cond, near_in, far_in, core, chip, near, planes):
    table = Table(near)
    level = lax.axis_index("depth")
    left = jnp.where(even("dom"), far_in[...], near_in[...]).reshape(8, 8, 128)
    right = jnp.where(even("dom"), near_in[...], far_in[...]).reshape(8, 8, 128)
    below = jnp.where(even("depth"), chip[...], core[...])
    above = jnp.where(even("depth"), core[...], chip[...])
    ghost_h = ghosts(head, left, right, 0, table)
    ghost_k = ghosts(cond, left, right, 1, table)
    for q in range(2):
        planes[2 * q, pl.ds(0, 32, stride=8), :] = below[32 * q : 32 * q + 32, :]
        planes[2 * q + 1, pl.ds(7, 32, stride=8), :] = above[32 * q : 32 * q + 32, :]
    level_k = iota((4, 8, 8, 128), 2)
    low = iota((8, 8, 128), 2) < 64

    def neighbours(x, ghost, q):
        around, y2, y3 = ghost
        x0, x3 = turn(x[0], 64), turn(x[3], 64)
        return [
            jnp.concatenate([jnp.where(low, around, x3)[None], x[:3]], axis=0),
            jnp.concatenate([x[1:], jnp.where(low, x0, around)[None]], axis=0),
            jnp.concatenate([y2[:, None], x[:, :7]], axis=1),
            jnp.concatenate([x[:, 1:], y3[:, None]], axis=1),
            jnp.where(level_k == 0, cube(planes[2 * q]), cube(turn(x.reshape(256, 128), 1, 0))),
            jnp.where(level_k == 7, cube(planes[2 * q + 1]), cube(turn(x.reshape(256, 128), 255, 0))),
        ]

    slab = iota((4, 8, 8, 128), 0)
    row_j = iota((4, 8, 8, 128), 1)
    lower = iota((4, 8, 8, 128), 3) < 64
    off_x, off_y = ~table.on_x, [~on for on in table.on_y]
    closed = [
        (slab == 0) & lower & off_x,
        (slab == 3) & ~lower & off_x,
        (row_j == 0) & off_y[0],
        (row_j == 7) & off_y[1],
        (level_k == 0) & (level == 0),
        (level_k == 7) & (level == lax.axis_size("depth") - 1),
    ]
    flux = total = None
    pairs = zip(neighbours(head, ghost_h, 0), neighbours(cond, ghost_k, 1), closed)
    for direction, (near_h, near_k, shut) in enumerate(pairs):
        face_k = jnp.where(shut, 0.0, cond + near_k)
        lift = (0.0, 0.0, 0.0, 0.0, -1.0, 1.0)[direction]
        part = jnp.where(shut, 0.0, face_k * (near_h - head + lift))
        flux = part if flux is None else flux + part
        total = face_k if total is None else total + face_k
    return 0.5 * flux, 0.5 * total


def newton_kernel(
    state, cond, water, near_in, far_in, core, chip, table, head_out, cond_out, water_out, near, far, to_core, to_chip, planes
):
    head = cube(state[0])
    flux, total = balance(head, cube(cond[...]), near_in, far_in, core, chip, table, planes)
    resid = cube(water[...]) - flux
    diagonal = 4.0 * cube(state[5]) * cube(state[2]) + total
    head_out[...] = (head - resid / diagonal).reshape(256, 128)
    new_cond, new_water = closure(head_out[...], *[state[f] for f in range(1, fields)])
    cond_out[...] = new_cond
    water_out[...] = new_water
    emit(head_out, cond_out, near, far, to_core, to_chip)


def leave(ref, cells):
    for c in range(2):
        turned = cells[128 * c : 128 * c + 128].T
        ref[0, :, 128 * c : 128 * c + 128] = turned[:blocks]
        ref[0, :, 128 * c + 256 : 128 * c + 384] = turned[blocks:]


def residual_kernel(head, cond, water, near_in, far_in, core, chip, table, head_out, resid_out, planes):
    flux, _ = balance(cube(head[...]), cube(cond[...]), near_in, far_in, core, chip, table, planes)
    leave(resid_out, water[...] - flux.reshape(256, 128))
    leave(head_out, head[...])


def shape(*dims):
    return jax.ShapeDtypeStruct(dims, f32)


def call(kernel, outs, scratch, *operands, space=pltpu.VMEM, limit=vmem):
    whole = pl.BlockSpec(memory_space=space)
    return pl.pallas_call(
        kernel,
        out_shape=outs,
        in_specs=[whole] * len(operands),
        out_specs=[whole] * len(outs),
        scratch_shapes=scratch,
        compiler_params=pltpu.CompilerParams(vmem_limit_bytes=limit),
    )(*operands)


def exchange(near, far, core, chip):
    lateral, columns = lax.axis_size("dom"), lax.axis_size("depth")

    def swap(x, partner):
        places = [(t, d) for t in range(lateral) for d in range(columns)]
        pairs = []
        for t, d in places:
            u, e = partner(t, d)
            pairs.append((t * columns + d, u * columns + e))
        return lax.ppermute(x, ("dom", "depth"), pairs)

    def far_of(t, d):
        u = ((t + 1) ^ 1) - 1
        return (u, d) if 0 <= u < lateral else (t, d ^ 1)

    def chip_of(t, d):
        e = ((d + 1) ^ 1) - 1
        return (t, e) if 0 <= e < columns else (t ^ 1, d)

    far = swap(far, far_of)
    near = swap(near, lambda t, d: (t ^ 1, d))
    chip = swap(chip, chip_of)
    core = swap(core, lambda t, d: (t, d ^ 1))
    return near, far, core, chip


def pack(head, water_prev, alpha, shape_n, theta_r, theta_s, sat_cond, refine, destination):
    outs = [shape(rows, blocks, 128), shape(peers, chunk, 128), shape(blocks, 128)]
    scratch = [pltpu.SMEM((blocks,), jnp.int32)] * 2 + [pltpu.VMEM((1, blocks, 512), f32)] * 7
    scratch += [pltpu.VMEM(out.shape, f32) for out in outs]
    scratch += [pltpu.VMEM((blocks * late, 128), f32), pltpu.VMEM((blocks * early, 128), f32)]
    scratch += [pltpu.VMEM((blocks, 128), jnp.int32), pltpu.SMEM((peers,), jnp.int32), pltpu.SMEM((blocks,), jnp.int32)]
    scratch += [pltpu.SemaphoreType.DMA((9,))] * 2
    operands = (refine, destination, alpha, shape_n, sat_cond, theta_s, theta_r, head, water_prev)
    return call(pack_kernel, outs, scratch, *operands, space=pltpu.HBM, limit=64 * 1024 * 1024)


def on_device(head, water_prev, alpha, shape_n, theta_r, theta_s, sat_cond, refine, destination, neighbours):
    own, send, stay = pack(head, water_prev, alpha, shape_n, theta_r, theta_s, sat_cond, refine, destination)
    recv = lax.all_to_all(send, "dom", 0, 0, tiled=True)
    (settled,) = call(settle_kernel, [shape(fields, 256, 128)], [], own, stay)
    near = neighbours.reshape(blocks, 16).T
    near = jnp.concatenate([near, near], axis=1)
    cells, halo = shape(256, 128), [shape(64, 128)] * 4
    state, cond, water, *outgoing = call(
        arrive_kernel,
        [shape(fields, 256, 128), cells, cells] + halo,
        [],
        recv.reshape(peers * chunk, 128), settled,
    )
    planes = [pltpu.VMEM((4, 256, 128), f32)]
    new_head, cond, water, *outgoing = call(
        newton_kernel, [cells] * 3 + halo, planes, state, cond, water, *exchange(*outgoing), near
    )
    final = shape(1, blocks, 512)
    return tuple(
        call(residual_kernel, [final, final], planes, new_head, cond, water, *exchange(*outgoing), near)
    )


def solution(mesh):
    cells = P("depth", "dom", None)
    return jax.shard_map(
        on_device,
        mesh=mesh,
        in_specs=(cells,) * 7 + (P("dom"), P("dom"), P("dom", None, None)),
        out_specs=(cells, cells),
        check_vma=False,
    )
```

```python
import jax
import jax.numpy as jnp
from jax import lax
from jax.experimental import pallas as pl
from jax.experimental.pallas import tpu as pltpu
from jax.sharding import PartitionSpec as P

peers = 16
blocks = 64
fields = 6
room = 4
reach = 16
rows = fields * 4
late, early = 16, 8
chunk = room * rows + 8
vmem = 48 * 1024 * 1024
f32 = jnp.float32


def lane_take(x, index):
    numbers = lax.GatherDimensionNumbers((), (1,), (1,), (0,), (0,))
    return lax.gather(x, index[..., None], numbers, (1, 1), mode=lax.GatherScatterMode.PROMISE_IN_BOUNDS)


def row_take(x, index):
    numbers = lax.GatherDimensionNumbers((), (0,), (0,), (1,), (1,))
    return lax.gather(x, index[..., None], numbers, (1, 1), mode=lax.GatherScatterMode.PROMISE_IN_BOUNDS)


def seat(device):
    return peers - 1 - ((device & 3) * 4 + (device >> 2))


def iota(shape, axis):
    return lax.broadcasted_iota(jnp.int32, shape, axis)


def turn(x, shift, axis=None):
    axis = x.ndim - 1 if axis is None else axis
    shift = shift % x.shape[axis]
    if shift == 0:
        return x
    if x.ndim == 2:
        return pltpu.roll(x, shift, axis)
    flat = pltpu.roll(x.reshape(-1, x.shape[-1]), shift, 1)
    return flat.reshape(x.shape)


def plane_weights(bit_y, bit_z):
    source, fine = iota((128, 128), 0), iota((128, 128), 1)

    def line(bit, shift):
        coarse, index = (source >> shift) & 7, (fine >> shift) & 7
        near = 4 * bit + (index >> 1)
        far = jnp.clip(near + 2 * (index & 1) - 1, 0, 7)
        return jnp.where(coarse == near, 0.75, 0.0) + jnp.where(coarse == far, 0.25, 0.0)

    weight = line(bit_y, 3) * line(bit_z, 0)
    return jnp.where((source >> 6) == (fine >> 6), weight, 0.0).astype(jnp.bfloat16)


def pack_kernel(*refs):
    sources, targets, refs = refs[:9], refs[9:12], refs[12:]
    held, (own, send, stay), refs = refs[:9], refs[9:12], refs[12:]
    work_late, work_early, weights, flags, count, slot_early, sems_in, sems_out = refs
    arriving = [pltpu.make_async_copy(source, ref, sems_in.at[n]) for n, (source, ref) in enumerate(zip(sources, held))]
    for copy in arriving:
        copy.start()
    leaving = []

    def depart(source, target):
        copy = pltpu.make_async_copy(source, target, sems_out.at[len(leaving)])
        copy.start()
        leaving.append(copy)

    for bits in range(4):
        table = plane_weights(bits // 2, bits % 2)
        for n in range(2):
            weights[128 * n : 128 * n + 128, 128 * bits : 128 * bits + 128] = table
    refine, destination = held[:2]
    me = lax.axis_index("dom")
    for peer in range(peers):
        count[peer] = 0
    arriving[0].wait()
    for block in range(blocks):
        flags[pl.ds(block, 1), :] = jnp.full((1, 128), refine[block], jnp.int32)
    lane = iota((blocks, 128), 1)
    half, fine_y, fine_z = (lane >> 6) & 1, (lane >> 3) & 7, lane & 7
    flag = flags[...]
    octant = jnp.maximum(flag - 1, 0)
    kept = flag == 0
    bit_x, bit_y, bit_z = (octant >> 2) & 1, (octant >> 1) & 1, octant & 1
    up_x = bit_x == 1

    def get(n):
        arriving[n].wait()
        return [held[n][0, :, 128 * c : 128 * c + 128] for c in range(4)]

    plain_y, plain_z = 4 * bit_y + (fine_y >> 1), 4 * bit_z + (fine_z >> 1)
    inner = plain_y * 8 + plain_z
    plain_index = [jnp.where(kept, lane, parity * 64 + inner) for parity in range(2)]

    def plain(v):
        chosen = [
            jnp.where(up_x, v[2], v[0]),
            jnp.where(kept, v[1], jnp.where(up_x, v[2], v[0])),
            jnp.where(kept, v[2], jnp.where(up_x, v[3], v[1])),
            jnp.where(kept | up_x, v[3], v[1]),
        ]
        return [lane_take(chosen[c], plain_index[c % 2]) for c in range(4)]

    lower = lane < 64

    def smooth(v):
        r = [turn(x, 64) for x in v]
        base = [jnp.where(up_x, v[2 + c], v[c]) for c in range(2)]
        base_r = [jnp.where(up_x, r[2 + c], r[c]) for c in range(2)]
        near = [
            jnp.where(lower, base[0], base_r[0]),
            jnp.where(lower, base_r[0], base[0]),
            jnp.where(lower, base[1], base_r[1]),
            jnp.where(lower, base_r[1], base[1]),
        ]
        far = [
            jnp.where(lower, jnp.where(up_x, r[1], v[0]), base[0]),
            jnp.where(lower, base[0], jnp.where(up_x, r[3], r[1])),
            jnp.where(lower, base_r[0], base[1]),
            jnp.where(lower, base[1], jnp.where(up_x, v[3], r[2])),
        ]
        x = jnp.concatenate([0.75 * near[c] + 0.25 * far[c] for c in range(4)], axis=0)
        high = x.astype(jnp.bfloat16)
        x = x - high.astype(f32)
        middle = x.astype(jnp.bfloat16)
        x = (x - middle.astype(f32)).astype(jnp.bfloat16)
        y = jnp.dot(jnp.concatenate([high, middle], axis=1), weights[...], preferred_element_type=f32)
        y = y + jnp.dot(x, weights[:128, :], preferred_element_type=f32)
        result = []
        for c in range(4):
            parts = [y[blocks * c : blocks * (c + 1), 128 * n : 128 * n + 128] for n in range(4)]
            parts = [jnp.where(bit_z == 1, parts[n + 1], parts[n]) for n in (0, 2)]
            result.append(jnp.where(kept, v[c], jnp.where(bit_y == 1, parts[1], parts[0])))
        return result

    def keep(f, values, work, size, first):
        for c in range(4):
            own[f * 4 + c] = values[c]
            for g in range(blocks // 8):
                work[pl.ds(8 * g * size + (f - first) * 4 + c, 8, stride=size), :] = values[c][8 * g : 8 * g + 8]
        depart(own.at[4 * f : 4 * f + 4], targets[0].at[4 * f : 4 * f + 4])

    for n, f in ((2, 2), (3, 3), (4, 4)):
        keep(f, plain(get(n)), work_late, late, 2)
    high, low = get(5), get(6)
    keep(5, plain([x - y for x, y in zip(high, low)]), work_late, late, 2)

    arriving[1].wait()
    for peer in range(peers):
        send[peer, rows * room :, :] = jnp.full((8, 128), -1.0, f32)
    for block in range(blocks):
        target = destination[block]
        owner = target >> 6
        place = seat(owner)
        used = count[owner] & (room - 1)
        count[owner] = used + 1
        spot = jnp.full((1, 128), target & 63, jnp.int32).astype(f32)
        slot_early[block] = room * late + used * early
        start = pl.ds(pl.multiple_of(used * late, 8), late)
        send[place, start, :] = work_late[block * late : block * late + late, :]
        send[place, pl.ds(room * rows + used, 1), :] = spot
        stay[block : block + 1, :] = jnp.where(owner == me, spot, -1.0)
    send[seat(me), rows * room :, :] = jnp.full((8, 128), -1.0, f32)
    depart(send.at[:, : room * late], targets[1].at[:, : room * late])
    depart(stay, targets[2])

    keep(0, smooth(get(7)), work_early, early, 0)
    keep(1, [x - y for x, y in zip(plain(low), smooth(get(8)))], work_early, early, 0)
    for block in range(blocks):
        start = pl.ds(pl.multiple_of(slot_early[block], 8), early)
        send[seat(destination[block] >> 6), start, :] = work_early[block * early : block * early + early, :]
    depart(send.at[:, room * late :], targets[1].at[:, room * late :])
    for copy in leaving:
        copy.wait()


def find(places):
    hit = places == (iota((blocks, 128), 1) & 63).astype(f32)
    row = jnp.sum(jnp.where(hit, iota((blocks, 128), 0), 0), axis=0, keepdims=True)
    has = jnp.sum(jnp.where(hit, 1, 0), axis=0, keepdims=True) > 0
    return row + (iota((1, 128), 1) & 64), has


def settle_kernel(own, stay, out):
    index, _ = find(stay[...])
    index = jnp.broadcast_to(index, (128, 128))
    for f in range(fields):
        for c in range(2):
            cells = jnp.concatenate([own[f * 4 + c], own[f * 4 + c + 2]], axis=0).T
            out[f, 128 * c : 128 * c + 128, :] = lane_take(cells, index)


def closure(head, less, alpha, shape_n, cond, span):
    expo = 1.0 - 1.0 / shape_n
    log_t = shape_n * jnp.log(alpha * jnp.maximum(-head, 0.0))
    log_s = jnp.log(1.0 + jnp.exp(log_t))
    root = jnp.exp(-0.5 * expo * log_s)
    inner = 1.0 - jnp.exp(expo * (log_t - log_s))
    return cond * root * inner * inner, 4.0 * (less + span * root * root)


def cube(x):
    return x.reshape(4, 8, 8, 128)


def face_tiles(x):
    y0, y7 = x[:, 0], x[:, 7]
    return [
        x[0],
        turn(x[3], 64),
        jnp.concatenate([y0, turn(y0, 64)], axis=0),
        jnp.concatenate([y7, turn(y7, 64)], axis=0),
    ]


def pack_faces(tiles_h, tiles_k, first):
    group = iota((8, 8, 128), 2) >> 4
    packed = None
    for f in range(4):
        for q, tiles in enumerate((tiles_h, tiles_k)):
            part = turn(tiles[f], (2 * f + q) * reach - first)
            packed = part if packed is None else jnp.where(group == 2 * f + q, part, packed)
    return packed.reshape(64, 128)


def even(axis):
    return lax.axis_index(axis) % 2 == 0


def emit(head_ref, cond_ref, near, far, core, chip):
    tiles_h, tiles_k = face_tiles(cube(head_ref[...])), face_tiles(cube(cond_ref[...]))
    right = pack_faces(tiles_h, tiles_k, blocks - reach)
    left = pack_faces(tiles_h, tiles_k, 0)
    near[...] = jnp.where(even("dom"), right, left)
    far[...] = jnp.where(even("dom"), left, right)
    for q, ref in enumerate((head_ref, cond_ref)):
        top, bottom = ref[pl.ds(7, 32, stride=8), :], ref[pl.ds(0, 32, stride=8), :]
        core[32 * q : 32 * q + 32, :] = jnp.where(even("depth"), top, bottom)
        chip[32 * q : 32 * q + 32, :] = jnp.where(even("depth"), bottom, top)


def arrive_kernel(recv, settled, head_out, state, cond_out, water_out, *outgoing):
    def slots(start):
        return [recv[pl.ds(start(o), peers, stride=chunk), :] for o in range(room)]

    places = jnp.concatenate(slots(lambda o: room * rows + o), axis=0)
    index, has = find(places)
    index = jnp.broadcast_to(index, (128, 128))
    for f in range(fields):
        for c in range(2):
            parts = []
            for r in (c, c + 2):
                if f < 2:
                    parts += slots(lambda o: room * late + o * early + f * 4 + r)
                else:
                    parts += slots(lambda o: o * late + (f - 2) * 4 + r)
            cells = jnp.concatenate(parts, axis=0).T
            span = slice(128 * c, 128 * c + 128)
            state[f, span, :] = jnp.where(has, lane_take(cells, index), settled[f, span, :])
    head_out[...] = state[0]
    cond, water = closure(*[state[f] for f in range(fields)])
    cond_out[...] = cond
    water_out[...] = water
    emit(state.at[0], cond_out, *outgoing)


class Table:
    def __init__(self, near):
        position = near[...] - lax.axis_index("dom") * blocks
        spot = jnp.where(position < 0, position + 80, jnp.where(position >= blocks, position + reach, position))
        present = near[...] >= 0
        spot = jnp.where(present, spot, 0)
        lower = iota((8, 128), 1) < 64
        front = iota((8, 128), 0) < 4

        def row(f, e):
            return jnp.broadcast_to(spot[4 * f + e : 4 * f + e + 1], (8, 128))

        def on(f, e):
            return jnp.broadcast_to(present[4 * f + e : 4 * f + e + 1].astype(jnp.int32), (8, 128)) == 1

        self.lower = lower
        self.one_x = jnp.where(lower, row(0, 0), row(1, 0))
        self.four_x = [
            jnp.where(
                lower,
                jnp.where(front, row(0, 2 * s), row(0, 2 * s + 1)),
                jnp.where(front, row(1, 2 * s), row(1, 2 * s + 1)),
            )
            for s in range(2)
        ]
        self.hang_x = (lower & on(0, 3)) | (~lower & on(1, 3))
        self.on_x = (lower & on(0, 0)) | (~lower & on(1, 0))
        self.one_y = [row(f, 0) for f in (2, 3)]
        self.four_y = [
            jnp.where(
                lower,
                jnp.where(front, row(f, 0), row(f, 1)),
                jnp.where(front, row(f, 2), row(f, 3)),
            )
            for f in (2, 3)
        ]
        self.hang_y = [on(f, 3) for f in (2, 3)]
        self.on_y = [on(f, 0) for f in (2, 3)]


def quarters(tile):
    pick = (iota((8, 128), 0) & 3) * 2
    result = []
    for a in range(4):
        pair = tile[2 * a] + tile[2 * a + 1]
        pair = 0.25 * (pair + turn(pair, 7, 0))
        result.append(row_take(pair, pick))
    return result


def ghosts(x, left, right, q, table):
    lane = iota((8, 8, 128), 2)
    tiles = []
    for f, tile in enumerate(face_tiles(x)):
        g = 2 * f + q
        after = jnp.where(lane < 80, turn(left, 64 - g * reach), turn(right, 80 - g * reach))
        tiles.append(jnp.where(lane < 64, tile, after))
    coarse = [quarters(tile) for tile in tiles]
    low = table.lower
    face_x = []
    for a in range(8):
        one = jnp.where(low, lane_take(tiles[1][a], table.one_x), lane_take(tiles[0][a], table.one_x))
        index = table.four_x[a // 4]
        four = jnp.where(low, lane_take(coarse[1][a % 4], index), lane_take(coarse[0][a % 4], index))
        face_x.append(jnp.where(table.hang_x, four, one))
    face_y = []
    for side, source in ((0, 3), (1, 2)):
        made = []
        for a in range(4):
            index = table.one_y[side]
            one = jnp.where(low, lane_take(tiles[source][a], index), lane_take(tiles[source][a + 4], index))
            four = lane_take(coarse[source][a], table.four_y[side])
            made.append(jnp.where(table.hang_y[side], four, one))
        face_y.append(jnp.stack(made))
    return jnp.stack(face_x), face_y[0], face_y[1]


def inside_kernel(head_ref, cond_ref, flux_out, total_out, *head_out):
    head, cond = cube(head_ref[...]), cube(cond_ref[...])
    lower = iota((8, 8, 128), 2) < 64
    level_k = iota((256, 128), 0) & 7

    def pair(k, other_k, h, other_h):
        face_k = k + other_k
        return face_k * (other_h - h), face_k

    def spread(below, above, sign):
        return [above[0]] + [above[n] + sign * below[n - 1] for n in range(1, len(above))] + [sign * below[-1]]

    steps = [pair(cond[n], cond[n + 1], head[n], head[n + 1]) for n in range(3)]
    cross = [jnp.where(lower, x, 0.0) for x in pair(cond[3], turn(cond[0], 64), head[3], turn(head[0], 64))]
    up_h, up_k = turn(head_ref[...], 255, 0), turn(cond_ref[...], 255, 0)
    rise = pair(cond_ref[...], up_k, head_ref[...], up_h + 1.0)
    rise = [jnp.where(level_k < 7, x, 0.0) for x in rise]
    along = pair(cond[:, :7], cond[:, 1:], head[:, :7], head[:, 1:])
    for q, (out, sign) in enumerate(((flux_out, -1.0), (total_out, 1.0))):
        x = spread([step[q] for step in steps], [step[q] for step in steps], sign)
        x[3] = x[3] + cross[q]
        x[0] = x[0] + sign * turn(cross[q], 64)
        empty = jnp.zeros((4, 1, 8, 128), f32)
        y = jnp.concatenate([along[q], empty], axis=1) + sign * jnp.concatenate([empty, along[q]], axis=1)
        z = rise[q] + sign * turn(rise[q], 1, 0)
        out[...] = (jnp.stack(x) + y).reshape(256, 128) + z
    for ref in head_out:
        leave(ref, head_ref[...])


def balance(head_ref, cond_ref, flux_in, total_in, near_in, far_in, core, chip, near, planes):
    table = Table(near)
    level = lax.axis_index("depth")
    head, cond = cube(head_ref[...]), cube(cond_ref[...])
    left = jnp.where(even("dom"), far_in[...], near_in[...]).reshape(8, 8, 128)
    right = jnp.where(even("dom"), near_in[...], far_in[...]).reshape(8, 8, 128)
    around_h, *sides_h = ghosts(head, left, right, 0, table)
    around_k, *sides_k = ghosts(cond, left, right, 1, table)
    lower = iota((8, 8, 128), 2) < 64

    def term(on, k, other_k, h, other_h):
        face_k = jnp.where(on, k + other_k, 0.0)
        return jnp.where(on, face_k * (other_h - h), 0.0), face_k

    edge_k, edge_h = jnp.where(lower, cond[0], cond[3]), jnp.where(lower, head[0], head[3])
    x = term(table.on_x, edge_k, around_k, edge_h, around_h)
    y = [term(table.on_y[n], cond[:, j], sides_k[n], head[:, j], sides_h[n]) for n, j in ((0, 0), (1, 7))]
    below = jnp.where(even("depth"), chip[...], core[...])
    above = jnp.where(even("depth"), core[...], chip[...])
    last = lax.axis_size("depth") - 1
    for n, (plane, k, on, lift) in enumerate(((below, 0, level > 0, -1.0), (above, 7, level < last, 1.0))):
        own_h, own_k = head_ref[pl.ds(k, 32, stride=8), :], cond_ref[pl.ds(k, 32, stride=8), :]
        for q, value in enumerate(term(on, own_k, plane[32:], own_h, plane[:32] + lift)):
            planes[2 * n + q, pl.ds(k, 32, stride=8), :] = value
    level_k = iota((4, 8, 8, 128), 2)
    sums = []
    for q, ref in enumerate((flux_in, total_in)):
        z = jnp.where(level_k == 0, cube(planes[q]), jnp.where(level_k == 7, cube(planes[2 + q]), 0.0))
        total = cube(ref[...]) + z
        slabs = [total[0] + jnp.where(lower, x[q], 0.0), total[1], total[2], total[3] + jnp.where(lower, 0.0, x[q])]
        total = jnp.stack(slabs)
        rows_j = [total[:, :1] + y[0][q][:, None], total[:, 1:7], total[:, 7:] + y[1][q][:, None]]
        sums.append(0.5 * jnp.concatenate(rows_j, axis=1))
    return sums


def newton_kernel(state, cond, water, flux, total, *refs):
    (near_in, far_in, core, chip, table), (head_out, cond_out, water_out, *outgoing), planes = refs[:5], refs[5:12], refs[12]
    flux, total = balance(state.at[0], cond, flux, total, near_in, far_in, core, chip, table, planes)
    resid = cube(water[...]) - flux
    diagonal = 4.0 * cube(state[5]) * cube(state[2]) + total
    head_out[...] = (cube(state[0]) - resid / diagonal).reshape(256, 128)
    new_cond, new_water = closure(head_out[...], *[state[f] for f in range(1, fields)])
    cond_out[...] = new_cond
    water_out[...] = new_water
    emit(head_out, cond_out, *outgoing)


def leave(ref, cells):
    for c in range(2):
        turned = cells[128 * c : 128 * c + 128].T
        ref[0, :, 128 * c : 128 * c + 128] = turned[:blocks]
        ref[0, :, 128 * c + 256 : 128 * c + 384] = turned[blocks:]


def residual_kernel(head, cond, water, flux, total, near_in, far_in, core, chip, table, resid_out, planes):
    flux, _ = balance(head, cond, flux, total, near_in, far_in, core, chip, table, planes)
    leave(resid_out, water[...] - flux.reshape(256, 128))


def shape(*dims):
    return jax.ShapeDtypeStruct(dims, f32)


def call(kernel, outs, scratch, *operands, space=pltpu.VMEM, limit=vmem):
    whole = pl.BlockSpec(memory_space=space)
    return pl.pallas_call(
        kernel,
        out_shape=outs,
        in_specs=[whole] * len(operands),
        out_specs=[whole] * len(outs),
        scratch_shapes=scratch,
        compiler_params=pltpu.CompilerParams(vmem_limit_bytes=limit),
    )(*operands)


def exchange(near, far, core, chip):
    lateral, columns = lax.axis_size("dom"), lax.axis_size("depth")

    def swap(x, partner):
        places = [(t, d) for t in range(lateral) for d in range(columns)]
        pairs = []
        for t, d in places:
            u, e = partner(t, d)
            pairs.append((t * columns + d, u * columns + e))
        return lax.ppermute(x, ("dom", "depth"), pairs)

    def far_of(t, d):
        u = ((t + 1) ^ 1) - 1
        return (u, d) if 0 <= u < lateral else (t, d ^ 1)

    def chip_of(t, d):
        e = ((d + 1) ^ 1) - 1
        return (t, e) if 0 <= e < columns else (t ^ 1, d)

    far = swap(far, far_of)
    near = swap(near, lambda t, d: (t ^ 1, d))
    chip = swap(chip, chip_of)
    core = swap(core, lambda t, d: (t, d ^ 1))
    return near, far, core, chip


def pack(head, water_prev, alpha, shape_n, theta_r, theta_s, sat_cond, refine, destination):
    outs = [shape(rows, blocks, 128), shape(peers, chunk, 128), shape(blocks, 128)]
    scratch = [pltpu.SMEM((blocks,), jnp.int32)] * 2 + [pltpu.VMEM((1, blocks, 512), f32)] * 7
    scratch += [pltpu.VMEM(out.shape, f32) for out in outs]
    scratch += [pltpu.VMEM((blocks * late, 128), f32), pltpu.VMEM((blocks * early, 128), f32)]
    scratch += [pltpu.VMEM((256, 512), jnp.bfloat16)]
    scratch += [pltpu.VMEM((blocks, 128), jnp.int32), pltpu.SMEM((peers,), jnp.int32), pltpu.SMEM((blocks,), jnp.int32)]
    scratch += [pltpu.SemaphoreType.DMA((9,))] * 2
    operands = (refine, destination, alpha, shape_n, sat_cond, theta_s, theta_r, head, water_prev)
    return call(pack_kernel, outs, scratch, *operands, space=pltpu.HBM, limit=64 * 1024 * 1024)


def on_device(head, water_prev, alpha, shape_n, theta_r, theta_s, sat_cond, refine, destination, neighbours):
    own, send, stay = pack(head, water_prev, alpha, shape_n, theta_r, theta_s, sat_cond, refine, destination)
    recv = lax.all_to_all(send, "dom", 0, 0, tiled=True, axis_index_groups=[sorted(range(peers), key=seat)])
    (settled,) = call(settle_kernel, [shape(fields, 256, 128)], [], own, stay)
    near = neighbours.reshape(blocks, 16).T
    near = jnp.concatenate([near, near], axis=1)
    cells, halo = shape(256, 128), [shape(64, 128)] * 4
    head, state, cond, water, *outgoing = call(
        arrive_kernel,
        [cells, shape(fields, 256, 128), cells, cells] + halo,
        [],
        recv.reshape(peers * chunk, 128), settled,
    )
    incoming = exchange(*outgoing)
    sums = call(inside_kernel, [cells, cells], [], head, cond)
    planes = [pltpu.VMEM((4, 256, 128), f32)]
    head, cond, water, *outgoing = call(
        newton_kernel, [cells] * 3 + halo, planes, state, cond, water, *sums, *incoming, near
    )
    incoming = exchange(*outgoing)
    final = shape(1, blocks, 512)
    *sums, new_head = call(inside_kernel, [cells, cells, final], [], head, cond)
    (residual,) = call(residual_kernel, [final], planes, head, cond, water, *sums, *incoming, near)
    return new_head, residual


def solution(mesh):
    cells = P("depth", "dom", None)
    return jax.shard_map(
        on_device,
        mesh=mesh,
        in_specs=(cells,) * 7 + (P("dom"), P("dom"), P("dom", None, None)),
        out_specs=(cells, cells),
        check_vma=False,
    )
```

```python
import jax
import jax.numpy as jnp
from jax import lax
from jax.experimental import pallas as pl
from jax.experimental.pallas import tpu as pltpu
from jax.sharding import PartitionSpec as P

peers = 16
blocks = 64
fields = 6
room = 4
reach = 16
rows = fields * 4
late, early = 16, 8
chunk = room * rows + 8
vmem = 48 * 1024 * 1024
f32 = jnp.float32


def lane_take(x, index):
    numbers = lax.GatherDimensionNumbers((), (1,), (1,), (0,), (0,))
    return lax.gather(x, index[..., None], numbers, (1, 1), mode=lax.GatherScatterMode.PROMISE_IN_BOUNDS)


def row_take(x, index):
    numbers = lax.GatherDimensionNumbers((), (0,), (0,), (1,), (1,))
    return lax.gather(x, index[..., None], numbers, (1, 1), mode=lax.GatherScatterMode.PROMISE_IN_BOUNDS)


def seat(device):
    return peers - 1 - ((device & 3) * 4 + (device >> 2))


def iota(shape, axis):
    return lax.broadcasted_iota(jnp.int32, shape, axis)


def turn(x, shift, axis=None):
    axis = x.ndim - 1 if axis is None else axis
    shift = shift % x.shape[axis]
    if shift == 0:
        return x
    if x.ndim == 2:
        return pltpu.roll(x, shift, axis)
    flat = pltpu.roll(x.reshape(-1, x.shape[-1]), shift, 1)
    return flat.reshape(x.shape)


def plane_weights(bit_y, bit_z):
    source, fine = iota((128, 128), 0), iota((128, 128), 1)

    def line(bit, shift):
        coarse, index = (source >> shift) & 7, (fine >> shift) & 7
        near = 4 * bit + (index >> 1)
        far = jnp.clip(near + 2 * (index & 1) - 1, 0, 7)
        return jnp.where(coarse == near, 0.75, 0.0) + jnp.where(coarse == far, 0.25, 0.0)

    weight = line(bit_y, 3) * line(bit_z, 0)
    return jnp.where((source >> 6) == (fine >> 6), weight, 0.0).astype(jnp.bfloat16)


def pack_kernel(*refs):
    sources, targets, refs = refs[:9], refs[9:12], refs[12:]
    held, refs = refs[:9], refs[9:]
    own, part_late, part_early, part_place, places, stay, *refs = refs
    work_late, work_early, weights, flags, free, taken, sems = refs
    arriving = [pltpu.make_async_copy(source, ref, sems.at[0]) for source, ref in zip(sources, held)]
    for copy in arriving:
        copy.start()
    leaving = []

    def depart(source, target):
        copy = pltpu.make_async_copy(source, target, sems.at[1])
        copy.start()
        leaving.append(copy)

    for bits in range(4):
        table = plane_weights(bits // 2, bits % 2)
        for n in range(3):
            weights[128 * n : 128 * n + 128, 128 * bits : 128 * bits + 128] = table
    refine, destination = held[:2]
    me = lax.axis_index("dom")
    for peer in range(peers):
        free[peer] = jnp.where(peer == me, peers * room * late, seat(peer) * room * late)
        part_place[peer] = jnp.full((8, 128), -1.0, f32)
    places[...] = jnp.full((2 * blocks, 128), -1, jnp.int32)
    for copy in arriving:
        copy.wait()
    for block in range(blocks):
        flags[pl.ds(block, 1), :] = jnp.full((1, 128), refine[block], jnp.int32)
    lane = iota((blocks, 128), 1)
    half, fine_y, fine_z = (lane >> 6) & 1, (lane >> 3) & 7, lane & 7
    flag = flags[...]
    octant = jnp.maximum(flag - 1, 0)
    kept = flag == 0
    bit_x, bit_y, bit_z = (octant >> 2) & 1, (octant >> 1) & 1, octant & 1
    up_x = bit_x == 1

    def get(n):
        return [held[n][0, :, 128 * c : 128 * c + 128] for c in range(4)]

    plain_y, plain_z = 4 * bit_y + (fine_y >> 1), 4 * bit_z + (fine_z >> 1)
    inner = plain_y * 8 + plain_z
    plain_index = [jnp.where(kept, lane, parity * 64 + inner) for parity in range(2)]

    def plain(v):
        chosen = [
            jnp.where(up_x, v[2], v[0]),
            jnp.where(kept, v[1], jnp.where(up_x, v[2], v[0])),
            jnp.where(kept, v[2], jnp.where(up_x, v[3], v[1])),
            jnp.where(kept | up_x, v[3], v[1]),
        ]
        return [lane_take(chosen[c], plain_index[c % 2]) for c in range(4)]

    lower = lane < 64

    def smooth(v):
        r = [turn(x, 64) for x in v]
        base = [jnp.where(up_x, v[2 + c], v[c]) for c in range(2)]
        base_r = [jnp.where(up_x, r[2 + c], r[c]) for c in range(2)]
        near = [
            jnp.where(lower, base[0], base_r[0]),
            jnp.where(lower, base_r[0], base[0]),
            jnp.where(lower, base[1], base_r[1]),
            jnp.where(lower, base_r[1], base[1]),
        ]
        far = [
            jnp.where(lower, jnp.where(up_x, r[1], v[0]), base[0]),
            jnp.where(lower, base[0], jnp.where(up_x, r[3], r[1])),
            jnp.where(lower, base_r[0], base[1]),
            jnp.where(lower, base[1], jnp.where(up_x, v[3], r[2])),
        ]
        x = jnp.concatenate([0.75 * near[c] + 0.25 * far[c] for c in range(4)], axis=0)
        high = x.astype(jnp.bfloat16)
        x = x - high.astype(f32)
        middle = x.astype(jnp.bfloat16)
        x = (x - middle.astype(f32)).astype(jnp.bfloat16)
        y = jnp.dot(jnp.concatenate([high, middle, x], axis=1), weights[...], preferred_element_type=f32)
        result = []
        for c in range(4):
            parts = [y[blocks * c : blocks * (c + 1), 128 * n : 128 * n + 128] for n in range(4)]
            parts = [jnp.where(bit_z == 1, parts[n + 1], parts[n]) for n in (0, 2)]
            result.append(jnp.where(kept, v[c], jnp.where(bit_y == 1, parts[1], parts[0])))
        return result

    def keep(f, values, work, size, first):
        for c in range(4):
            own[f * 4 + c] = values[c]
            for g in range(blocks // 8):
                work[pl.ds(8 * g * size + (f - first) * 4 + c, 8, stride=size), :] = values[c][8 * g : 8 * g + 8]
        depart(own.at[4 * f : 4 * f + 4], targets[0].at[4 * f : 4 * f + 4])

    low = get(6)
    keep(0, smooth(get(7)), work_early, early, 0)
    keep(1, [x - y for x, y in zip(plain(low), smooth(get(8)))], work_early, early, 0)
    for n, f in ((2, 2), (3, 3), (4, 4)):
        keep(f, plain(get(n)), work_late, late, 2)
    high = get(5)
    keep(5, plain([x - y for x, y in zip(high, low)]), work_late, late, 2)

    for block in range(blocks):
        target = destination[block]
        owner = target >> 6
        row = free[owner]
        free[owner] = row + late
        taken[block] = row >> 1
        place = jnp.full((1, 128), target, jnp.int32)
        part_late[pl.ds(pl.multiple_of(row, late), late), :] = work_late[block * late : block * late + late, :]
        places[pl.ds(row >> 4, 1), :] = place
        stay[block : block + 1, :] = place.astype(f32)
    for peer in range(peers):
        part_place[peer, :room, :] = places[room * peer : room * peer + room, :].astype(f32)
    depart(part_late.reshape(2 * peers, room * late, 128).at[:peers], targets[1].at[:, : room * late])
    depart(part_place, targets[1].at[:, room * rows :])
    depart(stay, targets[2])

    for block in range(blocks):
        row = pl.multiple_of(taken[block], early)
        part_early[pl.ds(row, early), :] = work_early[block * early : block * early + early, :]
    depart(part_early.reshape(2 * peers, room * early, 128).at[:peers], targets[1].at[:, room * late : room * rows])
    for copy in leaving:
        copy.wait()


def find(places):
    position = lax.axis_index("dom") * blocks + (iota((blocks, 128), 1) & 63)
    hit = places.astype(jnp.int32) == position
    row = jnp.sum(jnp.where(hit, iota((blocks, 128), 0), 0), axis=0, keepdims=True)
    has = jnp.sum(jnp.where(hit, 1, 0), axis=0, keepdims=True) > 0
    return row + (iota((1, 128), 1) & 64), has


def settle_kernel(own, stay, out):
    index, _ = find(stay[...])
    index = jnp.broadcast_to(index, (128, 128))
    for f in range(fields):
        for c in range(2):
            cells = jnp.concatenate([own[f * 4 + c], own[f * 4 + c + 2]], axis=0).T
            out[f, 128 * c : 128 * c + 128, :] = lane_take(cells, index)


def closure(head, alpha, shape_n, cond):
    expo = 1.0 - 1.0 / shape_n
    log_t = shape_n * jnp.log(alpha * jnp.maximum(-head, 0.0))
    log_s = jnp.log(1.0 + jnp.exp(log_t))
    root = jnp.exp(-0.5 * expo * log_s)
    inner = 1.0 - jnp.exp(expo * (log_t - log_s))
    return cond * root * inner * inner, root * root


def cube(x):
    return x.reshape(4, 8, 8, 128)


def face_tiles(x):
    y0, y7 = x[:, 0], x[:, 7]
    return [
        x[0],
        turn(x[3], 64),
        jnp.concatenate([y0, turn(y0, 64)], axis=0),
        jnp.concatenate([y7, turn(y7, 64)], axis=0),
    ]


def pack_faces(tiles_h, tiles_k):
    group = iota((8, 8, 128), 2) >> 4
    right = left = None
    for f in range(4):
        for q, tiles in enumerate((tiles_h, tiles_k)):
            g = 2 * f + q
            part = turn(tiles[f], g * reach)
            left = part if left is None else jnp.where(group == g, part, left)
            right = part if right is None else jnp.where(group == (g + 3) % 8, part, right)
    return right.reshape(64, 128), left.reshape(64, 128)


def even(axis):
    return lax.axis_index(axis) % 2 == 0


def emit(head_ref, cond_ref, near, far, core, chip):
    tiles_h, tiles_k = face_tiles(cube(head_ref[...])), face_tiles(cube(cond_ref[...]))
    right, left = pack_faces(tiles_h, tiles_k)
    near[...] = jnp.where(even("dom"), right, left)
    far[...] = jnp.where(even("dom"), left, right)
    for q, ref in enumerate((head_ref, cond_ref)):
        top, bottom = ref[pl.ds(7, 32, stride=8), :], ref[pl.ds(0, 32, stride=8), :]
        core[32 * q : 32 * q + 32, :] = jnp.where(even("depth"), top, bottom)
        chip[32 * q : 32 * q + 32, :] = jnp.where(even("depth"), bottom, top)


def receive(recv, settled, chosen):
    def slots(start):
        return [recv[pl.ds(start(o), peers, stride=chunk), :] for o in range(room)]

    places = jnp.concatenate(slots(lambda o: room * rows + o), axis=0)
    index, has = find(places)
    index = jnp.broadcast_to(index, (128, 128))
    for f in chosen:
        halves = []
        for c in range(2):
            parts = []
            for r in (c, c + 2):
                if f < 2:
                    parts += slots(lambda o: room * late + o * early + f * 4 + r)
                else:
                    parts += slots(lambda o: o * late + (f - 2) * 4 + r)
            cells = jnp.concatenate(parts, axis=0).T
            halves.append(jnp.where(has, lane_take(cells, index), settled[f, 128 * c : 128 * c + 128, :]))
        yield jnp.concatenate(halves, axis=0)


def arrive_kernel(recv, settled, head_out, alpha_out, shape_out, sat_out, cond_out, wet_out, *outgoing):
    outs = (head_out, alpha_out, shape_out, sat_out)
    for ref, value in zip(outs, receive(recv, settled, (0, 2, 3, 4))):
        ref[...] = value
    cond_out[...], wet_out[...] = closure(*[ref[...] for ref in outs])
    emit(head_out, cond_out, *outgoing)


def later_kernel(recv, settled, wet, less_out, span_out, water_out):
    for ref, value in zip((less_out, span_out), receive(recv, settled, (1, 5))):
        ref[...] = value
    water_out[...] = 4.0 * (less_out[...] + span_out[...] * wet[...])


class Table:
    def __init__(self, near):
        position = near[...] - lax.axis_index("dom") * blocks
        present = near[...] >= 0
        spot = jnp.where(present, position & 127, 0)
        lower = iota((8, 128), 1) < 64
        front = iota((8, 128), 0) < 4

        def row(f, e):
            return jnp.broadcast_to(spot[4 * f + e : 4 * f + e + 1], (8, 128))

        def on(f, e):
            return jnp.broadcast_to(present[4 * f + e : 4 * f + e + 1].astype(jnp.int32), (8, 128)) == 1

        self.lower = lower
        self.one_x = jnp.where(lower, row(0, 0), row(1, 0))
        self.four_x = [
            jnp.where(
                lower,
                jnp.where(front, row(0, 2 * s), row(0, 2 * s + 1)),
                jnp.where(front, row(1, 2 * s), row(1, 2 * s + 1)),
            )
            for s in range(2)
        ]
        self.hang_x = (lower & on(0, 3)) | (~lower & on(1, 3))
        self.on_x = (lower & on(0, 0)) | (~lower & on(1, 0))
        self.one_y = [row(f, 0) for f in (2, 3)]
        self.four_y = [
            jnp.where(
                lower,
                jnp.where(front, row(f, 0), row(f, 1)),
                jnp.where(front, row(f, 2), row(f, 3)),
            )
            for f in (2, 3)
        ]
        self.hang_y = [on(f, 3) for f in (2, 3)]
        self.on_y = [on(f, 0) for f in (2, 3)]


def quarters(tile):
    pick = (iota((8, 128), 0) & 3) * 2
    result = []
    for a in range(4):
        pair = tile[2 * a] + tile[2 * a + 1]
        pair = 0.25 * (pair + turn(pair, 7, 0))
        result.append(row_take(pair, pick))
    return result


def ghosts(x, left, right, q, table):
    lane = iota((8, 8, 128), 2)
    tiles = []
    for f, tile in enumerate(face_tiles(x)):
        g = 2 * f + q
        after = turn(jnp.where(lane >> 4 == g, right, left), (4 - g) * reach)
        tiles.append(jnp.where(lane < 64, tile, after))
    coarse = [quarters(tile) for tile in tiles]
    low = table.lower
    face_x = []
    for a in range(8):
        one = jnp.where(low, lane_take(tiles[1][a], table.one_x), lane_take(tiles[0][a], table.one_x))
        index = table.four_x[a // 4]
        four = jnp.where(low, lane_take(coarse[1][a % 4], index), lane_take(coarse[0][a % 4], index))
        face_x.append(jnp.where(table.hang_x, four, one))
    face_y = []
    for side, source in ((0, 3), (1, 2)):
        made = []
        for a in range(4):
            index = table.one_y[side]
            one = jnp.where(low, lane_take(tiles[source][a], index), lane_take(tiles[source][a + 4], index))
            four = lane_take(coarse[source][a], table.four_y[side])
            made.append(jnp.where(table.hang_y[side], four, one))
        face_y.append(jnp.stack(made))
    return jnp.stack(face_x), face_y[0], face_y[1]


def inside_kernel(head_ref, cond_ref, *outs):
    head, cond = cube(head_ref[...]), cube(cond_ref[...])
    lower = iota((8, 8, 128), 2) < 64
    level_k = iota((256, 128), 0) & 7

    def pair(k, other_k, h, other_h):
        face_k = k + other_k
        return face_k * (other_h - h), face_k

    def spread(below, above, sign):
        return [above[0]] + [above[n] + sign * below[n - 1] for n in range(1, len(above))] + [sign * below[-1]]

    steps = [pair(cond[n], cond[n + 1], head[n], head[n + 1]) for n in range(3)]
    cross = [jnp.where(lower, x, 0.0) for x in pair(cond[3], turn(cond[0], 64), head[3], turn(head[0], 64))]
    up_h, up_k = turn(head_ref[...], 255, 0), turn(cond_ref[...], 255, 0)
    rise = pair(cond_ref[...], up_k, head_ref[...], up_h + 1.0)
    rise = [jnp.where(level_k < 7, x, 0.0) for x in rise]
    along = pair(cond[:, :7], cond[:, 1:], head[:, :7], head[:, 1:])
    for q, (out, sign) in enumerate(zip(outs, (-1.0, 1.0))):
        x = spread([step[q] for step in steps], [step[q] for step in steps], sign)
        x[3] = x[3] + cross[q]
        x[0] = x[0] + sign * turn(cross[q], 64)
        empty = jnp.zeros((4, 1, 8, 128), f32)
        y = jnp.concatenate([along[q], empty], axis=1) + sign * jnp.concatenate([empty, along[q]], axis=1)
        z = rise[q] + sign * turn(rise[q], 1, 0)
        out[...] = (jnp.stack(x) + y).reshape(256, 128) + z


def last_inside_kernel(head_ref, cond_ref, flux_out, head_out):
    inside_kernel(head_ref, cond_ref, flux_out)
    leave(head_out, head_ref[...])


def balance(head_ref, cond_ref, sums_in, near_in, far_in, core, chip, near, planes):
    table = Table(near)
    level = lax.axis_index("depth")
    head, cond = cube(head_ref[...]), cube(cond_ref[...])
    left = jnp.where(even("dom"), far_in[...], near_in[...]).reshape(8, 8, 128)
    right = jnp.where(even("dom"), near_in[...], far_in[...]).reshape(8, 8, 128)
    around_h, *sides_h = ghosts(head, left, right, 0, table)
    around_k, *sides_k = ghosts(cond, left, right, 1, table)
    lower = iota((8, 8, 128), 2) < 64

    def term(on, k, other_k, h, other_h):
        face_k = jnp.where(on, k + other_k, 0.0)
        return jnp.where(on, face_k * (other_h - h), 0.0), face_k

    edge_k, edge_h = jnp.where(lower, cond[0], cond[3]), jnp.where(lower, head[0], head[3])
    x = term(table.on_x, edge_k, around_k, edge_h, around_h)
    y = [term(table.on_y[n], cond[:, j], sides_k[n], head[:, j], sides_h[n]) for n, j in ((0, 0), (1, 7))]
    below = jnp.where(even("depth"), chip[...], core[...])
    above = jnp.where(even("depth"), core[...], chip[...])
    last = lax.axis_size("depth") - 1
    for n, (plane, k, on, lift) in enumerate(((below, 0, level > 0, -1.0), (above, 7, level < last, 1.0))):
        own_h, own_k = head_ref[pl.ds(k, 32, stride=8), :], cond_ref[pl.ds(k, 32, stride=8), :]
        for q, value in enumerate(term(on, own_k, plane[32:], own_h, plane[:32] + lift)[: len(sums_in)]):
            planes[2 * n + q, pl.ds(k, 32, stride=8), :] = value
    level_k = iota((4, 8, 8, 128), 2)
    sums = []
    for q, ref in enumerate(sums_in):
        z = jnp.where(level_k == 0, cube(planes[q]), jnp.where(level_k == 7, cube(planes[2 + q]), 0.0))
        total = cube(ref[...]) + z
        slabs = [total[0] + jnp.where(lower, x[q], 0.0), total[1], total[2], total[3] + jnp.where(lower, 0.0, x[q])]
        total = jnp.stack(slabs)
        rows_j = [total[:, :1] + y[0][q][:, None], total[:, 1:7], total[:, 7:] + y[1][q][:, None]]
        sums.append(0.5 * jnp.concatenate(rows_j, axis=1))
    return sums


def newton_kernel(head, alpha, shape_n, sat, cond, span, water, flux, total, *refs):
    incoming, (head_out, cond_out, wet_out, *outgoing), planes = refs[:5], refs[5:12], refs[12]
    flux, total = balance(head, cond, (flux, total), *incoming, planes)
    resid = cube(water[...]) - flux
    diagonal = 4.0 * cube(span[...]) * cube(alpha[...]) + total
    head_out[...] = (cube(head[...]) - resid / diagonal).reshape(256, 128)
    cond_out[...], wet_out[...] = closure(head_out[...], alpha[...], shape_n[...], sat[...])
    emit(head_out, cond_out, *outgoing)


def leave(ref, cells):
    for c in range(2):
        turned = cells[128 * c : 128 * c + 128].T
        ref[0, :, 128 * c : 128 * c + 128] = turned[:blocks]
        ref[0, :, 128 * c + 256 : 128 * c + 384] = turned[blocks:]


def residual_kernel(head, cond, wet, less, span, flux, near_in, far_in, core, chip, table, resid_out, planes):
    (flux,) = balance(head, cond, (flux,), near_in, far_in, core, chip, table, planes)
    leave(resid_out, 4.0 * (less[...] + span[...] * wet[...]) - flux.reshape(256, 128))


def shape(*dims):
    return jax.ShapeDtypeStruct(dims, f32)


def call(kernel, outs, scratch, *operands, space=pltpu.VMEM, limit=vmem):
    whole = pl.BlockSpec(memory_space=space)
    return pl.pallas_call(
        kernel,
        out_shape=outs,
        in_specs=[whole] * len(operands),
        out_specs=[whole] * len(outs),
        scratch_shapes=scratch,
        compiler_params=pltpu.CompilerParams(vmem_limit_bytes=limit),
    )(*operands)


def exchange(near, far, core, chip):
    lateral, columns = lax.axis_size("dom"), lax.axis_size("depth")

    def swap(x, partner):
        places = [(t, d) for t in range(lateral) for d in range(columns)]
        pairs = []
        for t, d in places:
            u, e = partner(t, d)
            pairs.append((t * columns + d, u * columns + e))
        return lax.ppermute(x, ("dom", "depth"), pairs)

    def far_of(t, d):
        u = ((t + 1) ^ 1) - 1
        return (u, d) if 0 <= u < lateral else (t, d ^ 1)

    def chip_of(t, d):
        e = ((d + 1) ^ 1) - 1
        return (t, e) if 0 <= e < columns else (t ^ 1, d)

    far = swap(far, far_of)
    near = swap(near, lambda t, d: (t ^ 1, d))
    chip = swap(chip, chip_of)
    core = swap(core, lambda t, d: (t, d ^ 1))
    return near, far, core, chip


def pack(head, water_prev, alpha, shape_n, theta_r, theta_s, sat_cond, refine, destination):
    outs = [shape(rows, blocks, 128), shape(peers, chunk, 128), shape(blocks, 128)]
    scratch = [pltpu.SMEM((blocks,), jnp.int32)] * 2 + [pltpu.VMEM((1, blocks, 512), f32)] * 7
    scratch += [pltpu.VMEM((rows, blocks, 128), f32)]
    scratch += [pltpu.VMEM((2 * blocks * size, 128), f32) for size in (late, early)]
    scratch += [pltpu.VMEM((peers, 8, 128), f32), pltpu.VMEM((2 * blocks, 128), jnp.int32), pltpu.VMEM((blocks, 128), f32)]
    scratch += [pltpu.VMEM((blocks * late, 128), f32), pltpu.VMEM((blocks * early, 128), f32)]
    scratch += [pltpu.VMEM((384, 512), jnp.bfloat16)]
    scratch += [pltpu.VMEM((blocks, 128), jnp.int32), pltpu.SMEM((peers,), jnp.int32), pltpu.SMEM((blocks,), jnp.int32)]
    scratch += [pltpu.SemaphoreType.DMA((2,))]
    operands = (refine, destination, alpha, shape_n, sat_cond, theta_s, theta_r, head, water_prev)
    return call(pack_kernel, outs, scratch, *operands, space=pltpu.HBM, limit=64 * 1024 * 1024)


def on_device(head, water_prev, alpha, shape_n, theta_r, theta_s, sat_cond, refine, destination, neighbours):
    own, send, stay = pack(head, water_prev, alpha, shape_n, theta_r, theta_s, sat_cond, refine, destination)
    recv = lax.all_to_all(send, "dom", 0, 0, tiled=True, axis_index_groups=[sorted(range(peers), key=seat)])
    (settled,) = call(settle_kernel, [shape(fields, 256, 128)], [], own, stay)
    near = neighbours.reshape(blocks, 16).T
    near = jnp.concatenate([near, near], axis=1)
    cells, halo = shape(256, 128), [shape(64, 128)] * 4
    recv = recv.reshape(peers * chunk, 128)
    head, alpha, shape_n, sat, cond, wet, *outgoing = call(arrive_kernel, [cells] * 6 + halo, [], recv, settled)
    incoming = exchange(*outgoing)
    sums = call(inside_kernel, [cells, cells], [], head, cond)
    less, span, water = call(later_kernel, [cells] * 3, [], recv, settled, wet)
    planes = [pltpu.VMEM((4, 256, 128), f32)]
    head, cond, wet, *outgoing = call(
        newton_kernel, [cells] * 3 + halo, planes, head, alpha, shape_n, sat, cond, span, water, *sums, *incoming, near
    )
    incoming = exchange(*outgoing)
    final = shape(1, blocks, 512)
    flux, new_head = call(last_inside_kernel, [cells, final], [], head, cond)
    (residual,) = call(residual_kernel, [final], planes, head, cond, wet, less, span, flux, *incoming, near)
    return new_head, residual


def solution(mesh):
    cells = P("depth", "dom", None)
    return jax.shard_map(
        on_device,
        mesh=mesh,
        in_specs=(cells,) * 7 + (P("dom"), P("dom"), P("dom", None, None)),
        out_specs=(cells, cells),
        check_vma=False,
    )
```

```python
import jax
import jax.numpy as jnp
from jax import lax
from jax.experimental import pallas as pl
from jax.experimental.pallas import tpu as pltpu
from jax.sharding import PartitionSpec as P

peers = 16
blocks = 64
fields = 6
room = 4
reach = 16
rows = fields * 4
late, early = 16, 8
chunk = room * rows + 8
vmem = 48 * 1024 * 1024
f32 = jnp.float32


def lane_take(x, index):
    numbers = lax.GatherDimensionNumbers((), (1,), (1,), (0,), (0,))
    return lax.gather(x, index[..., None], numbers, (1, 1), mode=lax.GatherScatterMode.PROMISE_IN_BOUNDS)


def row_take(x, index):
    numbers = lax.GatherDimensionNumbers((), (0,), (0,), (1,), (1,))
    return lax.gather(x, index[..., None], numbers, (1, 1), mode=lax.GatherScatterMode.PROMISE_IN_BOUNDS)


def seat(device):
    return peers - 1 - ((device & 3) * 4 + (device >> 2))


def iota(shape, axis):
    return lax.broadcasted_iota(jnp.int32, shape, axis)


def turn(x, shift, axis=None):
    axis = x.ndim - 1 if axis is None else axis
    shift = shift % x.shape[axis]
    if shift == 0:
        return x
    if x.ndim == 2:
        return pltpu.roll(x, shift, axis)
    flat = pltpu.roll(x.reshape(-1, x.shape[-1]), shift, 1)
    return flat.reshape(x.shape)


def plane_weights(bit_y, bit_z):
    source, fine = iota((128, 128), 0), iota((128, 128), 1)

    def line(bit, shift):
        coarse, index = (source >> shift) & 7, (fine >> shift) & 7
        near = 4 * bit + (index >> 1)
        far = jnp.clip(near + 2 * (index & 1) - 1, 0, 7)
        return jnp.where(coarse == near, 0.75, 0.0) + jnp.where(coarse == far, 0.25, 0.0)

    weight = line(bit_y, 3) * line(bit_z, 0)
    return jnp.where((source >> 6) == (fine >> 6), weight, 0.0).astype(jnp.bfloat16)


def pack_kernel(*refs):
    sources, targets, refs = refs[:9], refs[9:12], refs[12:]
    held, refs = refs[:9], refs[9:]
    own, part_late, part_early, part_place, places, stay, *refs = refs
    work_late, work_early, weights, flags, free, taken, sems = refs
    arriving = [pltpu.make_async_copy(source, ref, sems.at[0]) for source, ref in zip(sources, held)]
    for copy in arriving:
        copy.start()
    leaving = []

    def depart(source, target):
        copy = pltpu.make_async_copy(source, target, sems.at[1])
        copy.start()
        leaving.append(copy)

    for bits in range(4):
        table = plane_weights(bits // 2, bits % 2)
        for n in range(3):
            weights[128 * n : 128 * n + 128, 128 * bits : 128 * bits + 128] = table
    refine, destination = held[:2]
    me = lax.axis_index("dom")
    for peer in range(peers):
        free[peer] = jnp.where(peer == me, peers * room * late, seat(peer) * room * late)
        part_place[peer] = jnp.full((8, 128), -1.0, f32)
    places[...] = jnp.full((2 * blocks, 128), -1, jnp.int32)
    for copy in arriving:
        copy.wait()
    for block in range(blocks):
        flags[pl.ds(block, 1), :] = jnp.full((1, 128), refine[block], jnp.int32)
    lane = iota((blocks, 128), 1)
    half, fine_y, fine_z = (lane >> 6) & 1, (lane >> 3) & 7, lane & 7
    flag = flags[...]
    octant = jnp.maximum(flag - 1, 0)
    kept = flag == 0
    bit_x, bit_y, bit_z = (octant >> 2) & 1, (octant >> 1) & 1, octant & 1
    up_x = bit_x == 1

    def get(n):
        return [held[n][0, :, 128 * c : 128 * c + 128] for c in range(4)]

    plain_y, plain_z = 4 * bit_y + (fine_y >> 1), 4 * bit_z + (fine_z >> 1)
    inner = plain_y * 8 + plain_z
    plain_index = [jnp.where(kept, lane, parity * 64 + inner) for parity in range(2)]

    def plain(v):
        chosen = [
            jnp.where(up_x, v[2], v[0]),
            jnp.where(kept, v[1], jnp.where(up_x, v[2], v[0])),
            jnp.where(kept, v[2], jnp.where(up_x, v[3], v[1])),
            jnp.where(kept | up_x, v[3], v[1]),
        ]
        return [lane_take(chosen[c], plain_index[c % 2]) for c in range(4)]

    lower = lane < 64

    def smooth(v):
        r = [turn(x, 64) for x in v]
        base = [jnp.where(up_x, v[2 + c], v[c]) for c in range(2)]
        base_r = [jnp.where(up_x, r[2 + c], r[c]) for c in range(2)]
        near = [
            jnp.where(lower, base[0], base_r[0]),
            jnp.where(lower, base_r[0], base[0]),
            jnp.where(lower, base[1], base_r[1]),
            jnp.where(lower, base_r[1], base[1]),
        ]
        far = [
            jnp.where(lower, jnp.where(up_x, r[1], v[0]), base[0]),
            jnp.where(lower, base[0], jnp.where(up_x, r[3], r[1])),
            jnp.where(lower, base_r[0], base[1]),
            jnp.where(lower, base[1], jnp.where(up_x, v[3], r[2])),
        ]
        x = jnp.concatenate([0.75 * near[c] + 0.25 * far[c] for c in range(4)], axis=0)
        high = x.astype(jnp.bfloat16)
        x = x - high.astype(f32)
        middle = x.astype(jnp.bfloat16)
        x = (x - middle.astype(f32)).astype(jnp.bfloat16)
        y = jnp.dot(jnp.concatenate([high, middle, x], axis=1), weights[...], preferred_element_type=f32)
        result = []
        for c in range(4):
            parts = [y[blocks * c : blocks * (c + 1), 128 * n : 128 * n + 128] for n in range(4)]
            parts = [jnp.where(bit_z == 1, parts[n + 1], parts[n]) for n in (0, 2)]
            result.append(jnp.where(kept, v[c], jnp.where(bit_y == 1, parts[1], parts[0])))
        return result

    def keep(f, values, work, size, first):
        for c in range(4):
            own[f * 4 + c] = values[c]
            for g in range(blocks // 8):
                work[pl.ds(8 * g * size + (f - first) * 4 + c, 8, stride=size), :] = values[c][8 * g : 8 * g + 8]
        depart(own.at[4 * f : 4 * f + 4], targets[0].at[4 * f : 4 * f + 4])

    low = get(6)
    keep(0, smooth(get(7)), work_early, early, 0)
    keep(1, [x - y for x, y in zip(plain(low), smooth(get(8)))], work_early, early, 0)
    for n, f in ((2, 2), (3, 3), (4, 4)):
        keep(f, plain(get(n)), work_late, late, 2)
    high = get(5)
    keep(5, plain([x - y for x, y in zip(high, low)]), work_late, late, 2)

    for block in range(blocks):
        target = destination[block]
        owner = target >> 6
        row = free[owner]
        free[owner] = row + late
        taken[block] = row >> 1
        place = jnp.full((1, 128), target, jnp.int32)
        part_late[pl.ds(pl.multiple_of(row, late), late), :] = work_late[block * late : block * late + late, :]
        places[pl.ds(row >> 4, 1), :] = place
        stay[block : block + 1, :] = place.astype(f32)
    for peer in range(peers):
        part_place[peer, :room, :] = places[room * peer : room * peer + room, :].astype(f32)
    depart(part_late.reshape(2 * peers, room * late, 128).at[:peers], targets[1].at[:, : room * late])
    depart(part_place, targets[1].at[:, room * rows :])
    depart(stay, targets[2])

    for block in range(blocks):
        row = pl.multiple_of(taken[block], early)
        part_early[pl.ds(row, early), :] = work_early[block * early : block * early + early, :]
    depart(part_early.reshape(2 * peers, room * early, 128).at[:peers], targets[1].at[:, room * late : room * rows])
    for copy in leaving:
        copy.wait()


def find(places):
    position = lax.axis_index("dom") * blocks + (iota((blocks, 128), 1) & 63)
    hit = places.astype(jnp.int32) == position
    row = jnp.sum(jnp.where(hit, iota((blocks, 128), 0), 0), axis=0, keepdims=True)
    has = jnp.sum(jnp.where(hit, 1, 0), axis=0, keepdims=True) > 0
    return row + (iota((1, 128), 1) & 64), has


def settle_kernel(own, stay, out):
    index, _ = find(stay[...])
    index = jnp.broadcast_to(index, (128, 128))
    for f in range(fields):
        for c in range(2):
            cells = jnp.concatenate([own[f * 4 + c], own[f * 4 + c + 2]], axis=0).T
            out[f, 128 * c : 128 * c + 128, :] = lane_take(cells, index)


def closure(head, alpha, shape_n, cond):
    expo = 1.0 - 1.0 / shape_n
    log_t = shape_n * jnp.log(alpha * jnp.maximum(-head, 0.0))
    log_s = jnp.log(1.0 + jnp.exp(log_t))
    root = jnp.exp(-0.5 * expo * log_s)
    inner = 1.0 - jnp.exp(expo * (log_t - log_s))
    return cond * root * inner * inner, root * root


def cube(x):
    return x.reshape(4, 8, 8, 128)


def face_tiles(x):
    y0, y7 = x[:, 0], x[:, 7]
    return [
        x[0],
        turn(x[3], 64),
        jnp.concatenate([y0, turn(y0, 64)], axis=0),
        jnp.concatenate([y7, turn(y7, 64)], axis=0),
    ]


def pack_faces(tiles_h, tiles_k):
    group = iota((8, 8, 128), 2) >> 4
    right = left = None
    for f in range(4):
        for q, tiles in enumerate((tiles_h, tiles_k)):
            g = 2 * f + q
            part = turn(tiles[f], g * reach)
            left = part if left is None else jnp.where(group == g, part, left)
            right = part if right is None else jnp.where(group == (g + 3) % 8, part, right)
    return right.reshape(64, 128), left.reshape(64, 128)


def even(axis):
    return lax.axis_index(axis) % 2 == 0


def emit(head_ref, cond_ref, near, far, core, chip):
    tiles_h, tiles_k = face_tiles(cube(head_ref[...])), face_tiles(cube(cond_ref[...]))
    right, left = pack_faces(tiles_h, tiles_k)
    near[...] = jnp.where(even("dom"), right, left)
    far[...] = jnp.where(even("dom"), left, right)
    for q, ref in enumerate((head_ref, cond_ref)):
        top, bottom = ref[pl.ds(7, 32, stride=8), :], ref[pl.ds(0, 32, stride=8), :]
        core[32 * q : 32 * q + 32, :] = jnp.where(even("depth"), top, bottom)
        chip[32 * q : 32 * q + 32, :] = jnp.where(even("depth"), bottom, top)


def receive(recv, settled, chosen):
    def slots(start):
        return [recv[pl.ds(start(o), peers, stride=chunk), :] for o in range(room)]

    places = jnp.concatenate(slots(lambda o: room * rows + o), axis=0)
    index, has = find(places)
    index = jnp.broadcast_to(index, (128, 128))
    for f in chosen:
        halves = []
        for c in range(2):
            parts = []
            for r in (c, c + 2):
                if f < 2:
                    parts += slots(lambda o: room * late + o * early + f * 4 + r)
                else:
                    parts += slots(lambda o: o * late + (f - 2) * 4 + r)
            cells = jnp.concatenate(parts, axis=0).T
            halves.append(jnp.where(has, lane_take(cells, index), settled[f, 128 * c : 128 * c + 128, :]))
        yield jnp.concatenate(halves, axis=0)


def arrive_kernel(recv, settled, head_out, alpha_out, shape_out, sat_out, cond_out, wet_out, *outgoing):
    outs = (head_out, alpha_out, shape_out, sat_out)
    for ref, value in zip(outs, receive(recv, settled, (0, 2, 3, 4))):
        ref[...] = value
    cond_out[...], wet_out[...] = closure(*[ref[...] for ref in outs])
    emit(head_out, cond_out, *outgoing)


def later_kernel(recv, settled, wet, less_out, span_out, water_out):
    for ref, value in zip((less_out, span_out), receive(recv, settled, (1, 5))):
        ref[...] = value
    water_out[...] = 4.0 * (less_out[...] + span_out[...] * wet[...])


class Table:
    def __init__(self, values):
        lower = iota((8, 128), 1) < 64
        front = iota((8, 128), 0) < 4

        def row(f, e):
            return jnp.broadcast_to(values[4 * f + e : 4 * f + e + 1], (8, 128))

        self.one_x = jnp.where(lower, row(0, 0), row(1, 0))
        self.four_x = [
            jnp.where(
                lower,
                jnp.where(front, row(0, 2 * s), row(0, 2 * s + 1)),
                jnp.where(front, row(1, 2 * s), row(1, 2 * s + 1)),
            )
            for s in range(2)
        ]
        self.one_y = [row(f, 0) for f in (2, 3)]
        self.four_y = [
            jnp.where(
                lower,
                jnp.where(front, row(f, 0), row(f, 1)),
                jnp.where(front, row(f, 2), row(f, 3)),
            )
            for f in (2, 3)
        ]
        self.last_x = jnp.where(lower, row(0, 3), row(1, 3))
        self.last_y = [row(f, 3) for f in (2, 3)]


class Faces:
    def __init__(self, near):
        position = near[...] - lax.axis_index("dom") * blocks
        self.position, self.present = position, near[...] >= 0
        self.own = (position >= 0) & (position < blocks)
        there = Table(self.present.astype(jnp.int32))
        self.on_x, self.hang_x = there.one_x == 1, there.last_x == 1
        self.on_y, self.hang_y = [x == 1 for x in there.one_y], [x == 1 for x in there.last_y]

    def own_lanes(self):
        return Table(jnp.where(self.present & self.own, self.position, 0))

    def halo_lanes(self, q):
        group = ((iota((16, 128), 0) >> 2) ^ 1) * 2 + q
        right = group * reach + self.position - blocks
        left = ((group + 3) & 7) * reach + self.position + reach
        return Table(jnp.where(self.present & ~self.own, jnp.where(self.position < 0, left, right), 0))

    def away(self):
        table = Table((self.present & ~self.own).astype(jnp.int32))
        x = [jnp.where(self.hang_x, four, table.one_x) == 1 for four in table.four_x]
        y = [jnp.where(self.hang_y[n], table.four_y[n], table.one_y[n]) == 1 for n in range(2)]
        return x, y


def quarters(tile):
    pick = (iota((8, 128), 0) & 3) * 2
    result = []
    for a in range(4):
        pair = tile[2 * a] + tile[2 * a + 1]
        pair = 0.25 * (pair + turn(pair, 7, 0))
        result.append(row_take(pair, pick))
    return result


def ghosts(faces, table, tiles, coarse):
    low = iota((8, 128), 1) < 64
    alike = len(tiles) == 1
    made = []

    def both(lists, n, index):
        if alike:
            return lane_take(lists[0][n], index)
        return jnp.where(low, lane_take(lists[1][n], index), lane_take(lists[0][n], index))

    for a in range(8):
        one = both(tiles, a, table.one_x)
        four = both(coarse, a % 4, table.four_x[a // 4])
        made.append(jnp.where(faces.hang_x, four, one))
    for side, source in ((0, 0 if alike else 3), (1, 0 if alike else 2)):
        for a in range(4):
            index = table.one_y[side]
            one = jnp.where(low, lane_take(tiles[source][a], index), lane_take(tiles[source][a + 4], index))
            four = lane_take(coarse[source][a], table.four_y[side])
            made.append(jnp.where(faces.hang_y[side], four, one))
    return made


def own_ghosts(refs, near, out):
    faces = Faces(near)
    table = faces.own_lanes()
    for q, ref in enumerate(refs):
        tiles = face_tiles(cube(ref[...]))
        for n, value in enumerate(ghosts(faces, table, tiles, [quarters(tile) for tile in tiles])):
            out[q, 8 * n : 8 * n + 8, :] = value


def all_ghosts(faces, left, right, own):
    group = iota((8, 8, 128), 2) >> 4
    away_x, away_y = faces.away()
    for q in range(2):
        tile = jnp.where(group % 2 == q, right, left)
        made = ghosts(faces, faces.halo_lanes(q), [tile], [quarters(tile)])
        away = [away_x[0]] * 4 + [away_x[1]] * 4 + [away_y[0]] * 4 + [away_y[1]] * 4
        made = [jnp.where(far, x, own[q, 8 * n : 8 * n + 8, :]) for n, (far, x) in enumerate(zip(away, made))]
        yield jnp.stack(made[:8]), jnp.stack(made[8:12]), jnp.stack(made[12:])


def inside_kernel(head_ref, cond_ref, near, own, *outs):
    own_ghosts((head_ref, cond_ref), near, own)
    head, cond = cube(head_ref[...]), cube(cond_ref[...])
    lower = iota((8, 8, 128), 2) < 64
    level_k = iota((256, 128), 0) & 7

    def pair(k, other_k, h, other_h):
        face_k = k + other_k
        return face_k * (other_h - h), face_k

    def spread(below, above, sign):
        return [above[0]] + [above[n] + sign * below[n - 1] for n in range(1, len(above))] + [sign * below[-1]]

    steps = [pair(cond[n], cond[n + 1], head[n], head[n + 1]) for n in range(3)]
    cross = [jnp.where(lower, x, 0.0) for x in pair(cond[3], turn(cond[0], 64), head[3], turn(head[0], 64))]
    up_h, up_k = turn(head_ref[...], 255, 0), turn(cond_ref[...], 255, 0)
    rise = pair(cond_ref[...], up_k, head_ref[...], up_h + 1.0)
    rise = [jnp.where(level_k < 7, x, 0.0) for x in rise]
    along = pair(cond[:, :7], cond[:, 1:], head[:, :7], head[:, 1:])
    for q, (out, sign) in enumerate(zip(outs, (-1.0, 1.0))):
        x = spread([step[q] for step in steps], [step[q] for step in steps], sign)
        x[3] = x[3] + cross[q]
        x[0] = x[0] + sign * turn(cross[q], 64)
        empty = jnp.zeros((4, 1, 8, 128), f32)
        y = jnp.concatenate([along[q], empty], axis=1) + sign * jnp.concatenate([empty, along[q]], axis=1)
        z = rise[q] + sign * turn(rise[q], 1, 0)
        out[...] = (jnp.stack(x) + y).reshape(256, 128) + z


def last_inside_kernel(head_ref, cond_ref, near, own, flux_out, head_out):
    inside_kernel(head_ref, cond_ref, near, own, flux_out)
    leave(head_out, head_ref[...])


def balance(head_ref, cond_ref, own, sums_in, near_in, far_in, core, chip, near, planes):
    table = Faces(near)
    level = lax.axis_index("depth")
    head, cond = cube(head_ref[...]), cube(cond_ref[...])
    left = jnp.where(even("dom"), far_in[...], near_in[...]).reshape(8, 8, 128)
    right = jnp.where(even("dom"), near_in[...], far_in[...]).reshape(8, 8, 128)
    (around_h, *sides_h), (around_k, *sides_k) = all_ghosts(table, left, right, own)
    lower = iota((8, 8, 128), 2) < 64

    def term(on, k, other_k, h, other_h):
        face_k = jnp.where(on, k + other_k, 0.0)
        return jnp.where(on, face_k * (other_h - h), 0.0), face_k

    edge_k, edge_h = jnp.where(lower, cond[0], cond[3]), jnp.where(lower, head[0], head[3])
    x = term(table.on_x, edge_k, around_k, edge_h, around_h)
    y = [term(table.on_y[n], cond[:, j], sides_k[n], head[:, j], sides_h[n]) for n, j in ((0, 0), (1, 7))]
    below = jnp.where(even("depth"), chip[...], core[...])
    above = jnp.where(even("depth"), core[...], chip[...])
    last = lax.axis_size("depth") - 1
    for n, (plane, k, on, lift) in enumerate(((below, 0, level > 0, -1.0), (above, 7, level < last, 1.0))):
        own_h, own_k = head_ref[pl.ds(k, 32, stride=8), :], cond_ref[pl.ds(k, 32, stride=8), :]
        for q, value in enumerate(term(on, own_k, plane[32:], own_h, plane[:32] + lift)[: len(sums_in)]):
            planes[2 * n + q, pl.ds(k, 32, stride=8), :] = value
    level_k = iota((4, 8, 8, 128), 2)
    sums = []
    for q, ref in enumerate(sums_in):
        z = jnp.where(level_k == 0, cube(planes[q]), jnp.where(level_k == 7, cube(planes[2 + q]), 0.0))
        total = cube(ref[...]) + z
        slabs = [total[0] + jnp.where(lower, x[q], 0.0), total[1], total[2], total[3] + jnp.where(lower, 0.0, x[q])]
        total = jnp.stack(slabs)
        rows_j = [total[:, :1] + y[0][q][:, None], total[:, 1:7], total[:, 7:] + y[1][q][:, None]]
        sums.append(0.5 * jnp.concatenate(rows_j, axis=1))
    return sums


def newton_kernel(head, alpha, shape_n, sat, cond, span, water, own, flux, total, *refs):
    incoming, (head_out, cond_out, wet_out, *outgoing), planes = refs[:5], refs[5:12], refs[12]
    flux, total = balance(head, cond, own, (flux, total), *incoming, planes)
    resid = cube(water[...]) - flux
    diagonal = 4.0 * cube(span[...]) * cube(alpha[...]) + total
    head_out[...] = (cube(head[...]) - resid / diagonal).reshape(256, 128)
    cond_out[...], wet_out[...] = closure(head_out[...], alpha[...], shape_n[...], sat[...])
    emit(head_out, cond_out, *outgoing)


def leave(ref, cells):
    for c in range(2):
        turned = cells[128 * c : 128 * c + 128].T
        ref[0, :, 128 * c : 128 * c + 128] = turned[:blocks]
        ref[0, :, 128 * c + 256 : 128 * c + 384] = turned[blocks:]


def residual_kernel(head, cond, wet, less, span, own, flux, near_in, far_in, core, chip, table, resid_out, planes):
    (flux,) = balance(head, cond, own, (flux,), near_in, far_in, core, chip, table, planes)
    leave(resid_out, 4.0 * (less[...] + span[...] * wet[...]) - flux.reshape(256, 128))


def shape(*dims):
    return jax.ShapeDtypeStruct(dims, f32)


def call(kernel, outs, scratch, *operands, space=pltpu.VMEM, limit=vmem):
    whole = pl.BlockSpec(memory_space=space)
    return pl.pallas_call(
        kernel,
        out_shape=outs,
        in_specs=[whole] * len(operands),
        out_specs=[whole] * len(outs),
        scratch_shapes=scratch,
        compiler_params=pltpu.CompilerParams(vmem_limit_bytes=limit),
    )(*operands)


def exchange(near, far, core, chip):
    lateral, columns = lax.axis_size("dom"), lax.axis_size("depth")

    def swap(x, partner):
        places = [(t, d) for t in range(lateral) for d in range(columns)]
        pairs = []
        for t, d in places:
            u, e = partner(t, d)
            pairs.append((t * columns + d, u * columns + e))
        return lax.ppermute(x, ("dom", "depth"), pairs)

    def far_of(t, d):
        u = ((t + 1) ^ 1) - 1
        return (u, d) if 0 <= u < lateral else (t, d ^ 1)

    def chip_of(t, d):
        e = ((d + 1) ^ 1) - 1
        return (t, e) if 0 <= e < columns else (t ^ 1, d)

    far = swap(far, far_of)
    near = swap(near, lambda t, d: (t ^ 1, d))
    chip = swap(chip, chip_of)
    core = swap(core, lambda t, d: (t, d ^ 1))
    return near, far, core, chip


def pack(head, water_prev, alpha, shape_n, theta_r, theta_s, sat_cond, refine, destination):
    outs = [shape(rows, blocks, 128), shape(peers, chunk, 128), shape(blocks, 128)]
    scratch = [pltpu.SMEM((blocks,), jnp.int32)] * 2 + [pltpu.VMEM((1, blocks, 512), f32)] * 7
    scratch += [pltpu.VMEM((rows, blocks, 128), f32)]
    scratch += [pltpu.VMEM((2 * blocks * size, 128), f32) for size in (late, early)]
    scratch += [pltpu.VMEM((peers, 8, 128), f32), pltpu.VMEM((2 * blocks, 128), jnp.int32), pltpu.VMEM((blocks, 128), f32)]
    scratch += [pltpu.VMEM((blocks * late, 128), f32), pltpu.VMEM((blocks * early, 128), f32)]
    scratch += [pltpu.VMEM((384, 512), jnp.bfloat16)]
    scratch += [pltpu.VMEM((blocks, 128), jnp.int32), pltpu.SMEM((peers,), jnp.int32), pltpu.SMEM((blocks,), jnp.int32)]
    scratch += [pltpu.SemaphoreType.DMA((2,))]
    operands = (refine, destination, alpha, shape_n, sat_cond, theta_s, theta_r, head, water_prev)
    return call(pack_kernel, outs, scratch, *operands, space=pltpu.HBM, limit=64 * 1024 * 1024)


def on_device(head, water_prev, alpha, shape_n, theta_r, theta_s, sat_cond, refine, destination, neighbours):
    held, send, stay = pack(head, water_prev, alpha, shape_n, theta_r, theta_s, sat_cond, refine, destination)
    recv = lax.all_to_all(send, "dom", 0, 0, tiled=True, axis_index_groups=[sorted(range(peers), key=seat)])
    (settled,) = call(settle_kernel, [shape(fields, 256, 128)], [], held, stay)
    near = neighbours.reshape(blocks, 16).T
    near = jnp.concatenate([near, near], axis=1)
    cells, halo = shape(256, 128), [shape(64, 128)] * 4
    recv = recv.reshape(peers * chunk, 128)
    head, alpha, shape_n, sat, cond, wet, *outgoing = call(arrive_kernel, [cells] * 6 + halo, [], recv, settled)
    incoming = exchange(*outgoing)
    ghost = shape(2, 128, 128)
    sums = call(inside_kernel, [ghost, cells, cells], [], head, cond, near)
    less, span, water = call(later_kernel, [cells] * 3, [], recv, settled, wet)
    planes = [pltpu.VMEM((4, 256, 128), f32)]
    head, cond, wet, *outgoing = call(
        newton_kernel, [cells] * 3 + halo, planes, head, alpha, shape_n, sat, cond, span, water, *sums, *incoming, near
    )
    incoming = exchange(*outgoing)
    final = shape(1, blocks, 512)
    own, flux, new_head = call(last_inside_kernel, [ghost, cells, final], [], head, cond, near)
    (residual,) = call(residual_kernel, [final], planes, head, cond, wet, less, span, own, flux, *incoming, near)
    return new_head, residual


def solution(mesh):
    cells = P("depth", "dom", None)
    return jax.shard_map(
        on_device,
        mesh=mesh,
        in_specs=(cells,) * 7 + (P("dom"), P("dom"), P("dom", None, None)),
        out_specs=(cells, cells),
        check_vma=False,
    )
```

```python
import jax
import jax.numpy as jnp
from jax import lax
from jax.experimental import pallas as pl
from jax.experimental.pallas import tpu as pltpu
from jax.sharding import PartitionSpec as P

peers = 16
blocks = 64
fields = 6
room = 4
reach = 16
rows = fields * 4
late, early = 16, 8
chunk = room * rows + 8
vmem = 48 * 1024 * 1024
f32 = jnp.float32


def lane_take(x, index):
    numbers = lax.GatherDimensionNumbers((), (1,), (1,), (0,), (0,))
    return lax.gather(x, index[..., None], numbers, (1, 1), mode=lax.GatherScatterMode.PROMISE_IN_BOUNDS)


def row_take(x, index):
    numbers = lax.GatherDimensionNumbers((), (0,), (0,), (1,), (1,))
    return lax.gather(x, index[..., None], numbers, (1, 1), mode=lax.GatherScatterMode.PROMISE_IN_BOUNDS)


def seat(device):
    return peers - 1 - ((device & 3) * 4 + (device >> 2))


def iota(shape, axis):
    return lax.broadcasted_iota(jnp.int32, shape, axis)


def turn(x, shift, axis=None):
    axis = x.ndim - 1 if axis is None else axis
    shift = shift % x.shape[axis]
    if shift == 0:
        return x
    if x.ndim == 2:
        return pltpu.roll(x, shift, axis)
    flat = pltpu.roll(x.reshape(-1, x.shape[-1]), shift, 1)
    return flat.reshape(x.shape)


def plane_weights(bit_y, bit_z):
    source, fine = iota((128, 128), 0), iota((128, 128), 1)

    def line(bit, shift):
        coarse, index = (source >> shift) & 7, (fine >> shift) & 7
        near = 4 * bit + (index >> 1)
        far = jnp.clip(near + 2 * (index & 1) - 1, 0, 7)
        return jnp.where(coarse == near, 0.75, 0.0) + jnp.where(coarse == far, 0.25, 0.0)

    weight = line(bit_y, 3) * line(bit_z, 0)
    return jnp.where((source >> 6) == (fine >> 6), weight, 0.0).astype(jnp.bfloat16)


def pack_kernel(*refs):
    sources, targets, refs = refs[:9], refs[9:12], refs[12:]
    held, refs = refs[:9], refs[9:]
    own, part_late, part_early, part_place, places, stay, *refs = refs
    work_late, work_early, weights, flags, free, taken, sems = refs
    arriving = [pltpu.make_async_copy(source, ref, sems.at[0]) for source, ref in zip(sources, held)]
    for copy in arriving:
        copy.start()
    leaving = []

    def depart(source, target):
        copy = pltpu.make_async_copy(source, target, sems.at[1])
        copy.start()
        leaving.append(copy)

    for bits in range(4):
        table = plane_weights(bits // 2, bits % 2)
        for n in range(3):
            weights[128 * n : 128 * n + 128, 128 * bits : 128 * bits + 128] = table
    refine, destination = held[:2]
    me = lax.axis_index("dom")
    for peer in range(peers):
        free[peer] = jnp.where(peer == me, peers * room * late, seat(peer) * room * late)
        part_place[peer] = jnp.full((8, 128), -1.0, f32)
    places[...] = jnp.full((2 * blocks, 128), -1, jnp.int32)
    for copy in arriving:
        copy.wait()
    for block in range(blocks):
        flags[pl.ds(block, 1), :] = jnp.full((1, 128), refine[block], jnp.int32)
    lane = iota((blocks, 128), 1)
    half, fine_y, fine_z = (lane >> 6) & 1, (lane >> 3) & 7, lane & 7
    flag = flags[...]
    octant = jnp.maximum(flag - 1, 0)
    kept = flag == 0
    bit_x, bit_y, bit_z = (octant >> 2) & 1, (octant >> 1) & 1, octant & 1
    up_x = bit_x == 1

    def get(n):
        return [held[n][0, :, 128 * c : 128 * c + 128] for c in range(4)]

    plain_y, plain_z = 4 * bit_y + (fine_y >> 1), 4 * bit_z + (fine_z >> 1)
    inner = plain_y * 8 + plain_z
    plain_index = [jnp.where(kept, lane, parity * 64 + inner) for parity in range(2)]

    def plain(v):
        chosen = [
            jnp.where(up_x, v[2], v[0]),
            jnp.where(kept, v[1], jnp.where(up_x, v[2], v[0])),
            jnp.where(kept, v[2], jnp.where(up_x, v[3], v[1])),
            jnp.where(kept | up_x, v[3], v[1]),
        ]
        return [lane_take(chosen[c], plain_index[c % 2]) for c in range(4)]

    lower = lane < 64

    def smooth(v):
        r = [turn(x, 64) for x in v]
        base = [jnp.where(up_x, v[2 + c], v[c]) for c in range(2)]
        base_r = [jnp.where(up_x, r[2 + c], r[c]) for c in range(2)]
        near = [
            jnp.where(lower, base[0], base_r[0]),
            jnp.where(lower, base_r[0], base[0]),
            jnp.where(lower, base[1], base_r[1]),
            jnp.where(lower, base_r[1], base[1]),
        ]
        far = [
            jnp.where(lower, jnp.where(up_x, r[1], v[0]), base[0]),
            jnp.where(lower, base[0], jnp.where(up_x, r[3], r[1])),
            jnp.where(lower, base_r[0], base[1]),
            jnp.where(lower, base[1], jnp.where(up_x, v[3], r[2])),
        ]
        x = jnp.concatenate([0.75 * near[c] + 0.25 * far[c] for c in range(4)], axis=0)
        high = x.astype(jnp.bfloat16)
        x = x - high.astype(f32)
        middle = x.astype(jnp.bfloat16)
        x = (x - middle.astype(f32)).astype(jnp.bfloat16)
        y = jnp.dot(jnp.concatenate([high, middle, x], axis=1), weights[...], preferred_element_type=f32)
        result = []
        for c in range(4):
            parts = [y[blocks * c : blocks * (c + 1), 128 * n : 128 * n + 128] for n in range(4)]
            parts = [jnp.where(bit_z == 1, parts[n + 1], parts[n]) for n in (0, 2)]
            result.append(jnp.where(kept, v[c], jnp.where(bit_y == 1, parts[1], parts[0])))
        return result

    def keep(f, values, work, size, first):
        for c in range(4):
            own[f * 4 + c] = values[c]
            for g in range(blocks // 8):
                work[pl.ds(8 * g * size + (f - first) * 4 + c, 8, stride=size), :] = values[c][8 * g : 8 * g + 8]
        depart(own.at[4 * f : 4 * f + 4], targets[0].at[4 * f : 4 * f + 4])

    low = get(6)
    keep(0, smooth(get(7)), work_early, early, 0)
    keep(1, [x - y for x, y in zip(plain(low), smooth(get(8)))], work_early, early, 0)
    for n, f in ((2, 2), (3, 3), (4, 4)):
        keep(f, plain(get(n)), work_late, late, 2)
    high = get(5)
    keep(5, plain([x - y for x, y in zip(high, low)]), work_late, late, 2)

    for block in range(blocks):
        target = destination[block]
        owner = target >> 6
        row = free[owner]
        free[owner] = row + late
        taken[block] = row >> 1
        place = jnp.full((1, 128), target, jnp.int32)
        part_late[pl.ds(pl.multiple_of(row, late), late), :] = work_late[block * late : block * late + late, :]
        places[pl.ds(row >> 4, 1), :] = place
        stay[block : block + 1, :] = place.astype(f32)
    for peer in range(peers):
        part_place[peer, :room, :] = places[room * peer : room * peer + room, :].astype(f32)
    depart(part_late.reshape(2 * peers, room * late, 128).at[:peers], targets[1].at[:, : room * late])
    depart(part_place, targets[1].at[:, room * rows :])
    depart(stay, targets[2])

    for block in range(blocks):
        row = pl.multiple_of(taken[block], early)
        part_early[pl.ds(row, early), :] = work_early[block * early : block * early + early, :]
    depart(part_early.reshape(2 * peers, room * early, 128).at[:peers], targets[1].at[:, room * late : room * rows])
    for copy in leaving:
        copy.wait()


def find(places):
    position = lax.axis_index("dom") * blocks + (iota((blocks, 128), 1) & 63)
    hit = places.astype(jnp.int32) == position
    row = jnp.sum(jnp.where(hit, iota((blocks, 128), 0), 0), axis=0, keepdims=True)
    has = jnp.sum(jnp.where(hit, 1, 0), axis=0, keepdims=True) > 0
    return row + (iota((1, 128), 1) & 64), has


def settle_kernel(own, stay, out):
    index, _ = find(stay[...])
    index = jnp.broadcast_to(index, (128, 128))
    for f in range(fields):
        for c in range(2):
            cells = jnp.concatenate([own[f * 4 + c], own[f * 4 + c + 2]], axis=0).T
            out[f, 128 * c : 128 * c + 128, :] = lane_take(cells, index)


def closure(head, alpha, shape_n, cond):
    expo = 1.0 - 1.0 / shape_n
    log_t = shape_n * jnp.log(alpha * jnp.maximum(-head, 0.0))
    log_s = jnp.log(1.0 + jnp.exp(log_t))
    root = jnp.exp(-0.5 * expo * log_s)
    inner = 1.0 - jnp.exp(expo * (log_t - log_s))
    return cond * root * inner * inner, root * root


def cube(x):
    return x.reshape(4, 8, 8, 128)


def face_tiles(x):
    y0, y7 = x[:, 0], x[:, 7]
    return [
        x[0],
        turn(x[3], 64),
        jnp.concatenate([y0, turn(y0, 64)], axis=0),
        jnp.concatenate([y7, turn(y7, 64)], axis=0),
    ]


def pack_faces(head, cond):
    group = iota((8, 8, 128), 2) >> 4
    right = left = None
    for f in range(4):
        for q, x in enumerate((head, cond)):
            g = 2 * f + q
            if f < 2:
                part = turn(x[3 * f], 64 * f + g * reach)
            else:
                edge = x[:, 7 * (f - 2)]
                part = jnp.concatenate([turn(edge, g * reach), turn(edge, 64 + g * reach)], axis=0)
            left = part if left is None else jnp.where(group == g, part, left)
            right = part if right is None else jnp.where(group == (g + 3) % 8, part, right)
    return right.reshape(64, 128), left.reshape(64, 128)


def even(axis):
    return lax.axis_index(axis) % 2 == 0


def emit(head_ref, cond_ref, near, far, core, chip):
    right, left = pack_faces(cube(head_ref[...]), cube(cond_ref[...]))
    near[...] = jnp.where(even("dom"), right, left)
    far[...] = jnp.where(even("dom"), left, right)
    for q, ref in enumerate((head_ref, cond_ref)):
        top, bottom = ref[pl.ds(7, 32, stride=8), :], ref[pl.ds(0, 32, stride=8), :]
        core[32 * q : 32 * q + 32, :] = jnp.where(even("depth"), top, bottom)
        chip[32 * q : 32 * q + 32, :] = jnp.where(even("depth"), bottom, top)


def receive(recv, settled, chosen):
    def slots(start):
        return [recv[pl.ds(start(o), peers, stride=chunk), :] for o in range(room)]

    places = jnp.concatenate(slots(lambda o: room * rows + o), axis=0)
    index, has = find(places)
    index = jnp.broadcast_to(index, (128, 128))
    for f in chosen:
        halves = []
        for c in range(2):
            parts = []
            for r in (c, c + 2):
                if f < 2:
                    parts += slots(lambda o: room * late + o * early + f * 4 + r)
                else:
                    parts += slots(lambda o: o * late + (f - 2) * 4 + r)
            cells = jnp.concatenate(parts, axis=0).T
            halves.append(jnp.where(has, lane_take(cells, index), settled[f, 128 * c : 128 * c + 128, :]))
        yield jnp.concatenate(halves, axis=0)


def arrive_kernel(recv, settled, head_out, alpha_out, shape_out, sat_out, cond_out, wet_out, *outgoing):
    outs = (head_out, alpha_out, shape_out, sat_out)
    for ref, value in zip(outs, receive(recv, settled, (0, 2, 3, 4))):
        ref[...] = value
    cond_out[...], wet_out[...] = closure(*[ref[...] for ref in outs])
    emit(head_out, cond_out, *outgoing)


def later_kernel(recv, settled, wet, less_out, span_out, water_out):
    for ref, value in zip((less_out, span_out), receive(recv, settled, (1, 5))):
        ref[...] = value
    water_out[...] = 4.0 * (less_out[...] + span_out[...] * wet[...])


class Table:
    def __init__(self, values):
        lower = iota((8, 128), 1) < 64
        front = iota((8, 128), 0) < 4

        def row(f, e):
            return jnp.broadcast_to(values[4 * f + e : 4 * f + e + 1], (8, 128))

        self.one_x = jnp.where(lower, row(0, 0), row(1, 0))
        self.four_x = [
            jnp.where(
                lower,
                jnp.where(front, row(0, 2 * s), row(0, 2 * s + 1)),
                jnp.where(front, row(1, 2 * s), row(1, 2 * s + 1)),
            )
            for s in range(2)
        ]
        self.one_y = [row(f, 0) for f in (2, 3)]
        self.four_y = [
            jnp.where(
                lower,
                jnp.where(front, row(f, 0), row(f, 1)),
                jnp.where(front, row(f, 2), row(f, 3)),
            )
            for f in (2, 3)
        ]
        self.last_x = jnp.where(lower, row(0, 3), row(1, 3))
        self.last_y = [row(f, 3) for f in (2, 3)]


class Faces:
    def __init__(self, near):
        position = near[...] - lax.axis_index("dom") * blocks
        self.position, self.present = position, near[...] >= 0
        self.own = (position >= 0) & (position < blocks)
        there = Table(self.present.astype(jnp.int32))
        self.on_x, self.hang_x = there.one_x == 1, there.last_x == 1
        self.on_y, self.hang_y = [x == 1 for x in there.one_y], [x == 1 for x in there.last_y]

    def own_lanes(self):
        return Table(jnp.where(self.present & self.own, self.position, 0))

    def halo_lanes(self, q):
        group = ((iota((16, 128), 0) >> 2) ^ 1) * 2 + q
        right = group * reach + self.position - blocks
        left = ((group + 3) & 7) * reach + self.position + reach
        return Table(jnp.where(self.present & ~self.own, jnp.where(self.position < 0, left, right), 0))

    def away(self):
        table = Table((self.present & ~self.own).astype(jnp.int32))
        x = [jnp.where(self.hang_x, four, table.one_x) == 1 for four in table.four_x]
        y = [jnp.where(self.hang_y[n], table.four_y[n], table.one_y[n]) == 1 for n in range(2)]
        return x, y


def quarters(tile):
    pick = (iota((8, 128), 0) & 3) * 2
    result = []
    for a in range(4):
        pair = tile[2 * a] + tile[2 * a + 1]
        pair = 0.25 * (pair + turn(pair, 7, 0))
        result.append(row_take(pair, pick))
    return result


def ghosts(faces, table, tiles, coarse):
    low = iota((8, 128), 1) < 64
    alike = len(tiles) == 1
    made = []

    def both(lists, n, index):
        if alike:
            return lane_take(lists[0][n], index)
        return jnp.where(low, lane_take(lists[1][n], index), lane_take(lists[0][n], index))

    for a in range(8):
        one = both(tiles, a, table.one_x)
        four = both(coarse, a % 4, table.four_x[a // 4])
        made.append(jnp.where(faces.hang_x, four, one))
    for side, source in ((0, 0 if alike else 3), (1, 0 if alike else 2)):
        for a in range(4):
            index = table.one_y[side]
            one = jnp.where(low, lane_take(tiles[source][a], index), lane_take(tiles[source][a + 4], index))
            four = lane_take(coarse[source][a], table.four_y[side])
            made.append(jnp.where(faces.hang_y[side], four, one))
    return made


def own_ghosts(refs, near, out):
    faces = Faces(near)
    table = faces.own_lanes()
    for q, ref in enumerate(refs):
        tiles = face_tiles(cube(ref[...]))
        for n, value in enumerate(ghosts(faces, table, tiles, [quarters(tile) for tile in tiles])):
            out[q, 8 * n : 8 * n + 8, :] = value


def all_ghosts(faces, left, right, own):
    group = iota((8, 8, 128), 2) >> 4
    away_x, away_y = faces.away()
    for q in range(2):
        tile = jnp.where(group % 2 == q, right, left)
        made = ghosts(faces, faces.halo_lanes(q), [tile], [quarters(tile)])
        away = [away_x[0]] * 4 + [away_x[1]] * 4 + [away_y[0]] * 4 + [away_y[1]] * 4
        made = [jnp.where(far, x, own[q, 8 * n : 8 * n + 8, :]) for n, (far, x) in enumerate(zip(away, made))]
        yield jnp.stack(made[:8]), jnp.stack(made[8:12]), jnp.stack(made[12:])


def inside_kernel(head_ref, cond_ref, near, own, *outs):
    own_ghosts((head_ref, cond_ref), near, own)
    head, cond = cube(head_ref[...]), cube(cond_ref[...])
    lower = iota((8, 8, 128), 2) < 64
    level_k = iota((256, 128), 0) & 7

    def pair(k, other_k, h, other_h):
        face_k = k + other_k
        return face_k * (other_h - h), face_k

    def spread(below, above, sign):
        return [above[0]] + [above[n] + sign * below[n - 1] for n in range(1, len(above))] + [sign * below[-1]]

    steps = [pair(cond[n], cond[n + 1], head[n], head[n + 1]) for n in range(3)]
    cross = [jnp.where(lower, x, 0.0) for x in pair(cond[3], turn(cond[0], 64), head[3], turn(head[0], 64))]
    up_h, up_k = turn(head_ref[...], 255, 0), turn(cond_ref[...], 255, 0)
    rise = pair(cond_ref[...], up_k, head_ref[...], up_h + 1.0)
    rise = [jnp.where(level_k < 7, x, 0.0) for x in rise]
    along = pair(cond[:, :7], cond[:, 1:], head[:, :7], head[:, 1:])
    for q, (out, sign) in enumerate(zip(outs, (-1.0, 1.0))):
        x = spread([step[q] for step in steps], [step[q] for step in steps], sign)
        x[3] = x[3] + cross[q]
        x[0] = x[0] + sign * turn(cross[q], 64)
        empty = jnp.zeros((4, 1, 8, 128), f32)
        y = jnp.concatenate([along[q], empty], axis=1) + sign * jnp.concatenate([empty, along[q]], axis=1)
        z = rise[q] + sign * turn(rise[q], 1, 0)
        out[...] = (jnp.stack(x) + y).reshape(256, 128) + z


def last_inside_kernel(head_ref, cond_ref, near, own, flux_out, head_out):
    inside_kernel(head_ref, cond_ref, near, own, flux_out)
    leave(head_out, head_ref[...])


def balance(head_ref, cond_ref, own, sums_in, near_in, far_in, core, chip, near, planes):
    table = Faces(near)
    level = lax.axis_index("depth")
    head, cond = cube(head_ref[...]), cube(cond_ref[...])
    left = jnp.where(even("dom"), far_in[...], near_in[...]).reshape(8, 8, 128)
    right = jnp.where(even("dom"), near_in[...], far_in[...]).reshape(8, 8, 128)
    (around_h, *sides_h), (around_k, *sides_k) = all_ghosts(table, left, right, own)
    lower = iota((8, 8, 128), 2) < 64

    def term(on, k, other_k, h, other_h):
        face_k = jnp.where(on, k + other_k, 0.0)
        return jnp.where(on, face_k * (other_h - h), 0.0), face_k

    edge_k, edge_h = jnp.where(lower, cond[0], cond[3]), jnp.where(lower, head[0], head[3])
    x = term(table.on_x, edge_k, around_k, edge_h, around_h)
    y = [term(table.on_y[n], cond[:, j], sides_k[n], head[:, j], sides_h[n]) for n, j in ((0, 0), (1, 7))]
    below = jnp.where(even("depth"), chip[...], core[...])
    above = jnp.where(even("depth"), core[...], chip[...])
    last = lax.axis_size("depth") - 1
    for n, (plane, k, on, lift) in enumerate(((below, 0, level > 0, -1.0), (above, 7, level < last, 1.0))):
        own_h, own_k = head_ref[pl.ds(k, 32, stride=8), :], cond_ref[pl.ds(k, 32, stride=8), :]
        for q, value in enumerate(term(on, own_k, plane[32:], own_h, plane[:32] + lift)[: len(sums_in)]):
            planes[2 * n + q, pl.ds(k, 32, stride=8), :] = value
    level_k = iota((4, 8, 8, 128), 2)
    sums = []
    for q, ref in enumerate(sums_in):
        z = jnp.where(level_k == 0, cube(planes[q]), jnp.where(level_k == 7, cube(planes[2 + q]), 0.0))
        total = cube(ref[...]) + z
        slabs = [total[0] + jnp.where(lower, x[q], 0.0), total[1], total[2], total[3] + jnp.where(lower, 0.0, x[q])]
        total = jnp.stack(slabs)
        rows_j = [total[:, :1] + y[0][q][:, None], total[:, 1:7], total[:, 7:] + y[1][q][:, None]]
        sums.append(0.5 * jnp.concatenate(rows_j, axis=1))
    return sums


def newton_kernel(head, alpha, shape_n, sat, cond, span, water, own, flux, total, *refs):
    incoming, (head_out, cond_out, wet_out, *outgoing), planes = refs[:5], refs[5:12], refs[12]
    flux, total = balance(head, cond, own, (flux, total), *incoming, planes)
    resid = cube(water[...]) - flux
    diagonal = 4.0 * cube(span[...]) * cube(alpha[...]) + total
    head_out[...] = (cube(head[...]) - resid / diagonal).reshape(256, 128)
    cond_out[...], wet_out[...] = closure(head_out[...], alpha[...], shape_n[...], sat[...])
    emit(head_out, cond_out, *outgoing)


def leave(ref, cells):
    for c in range(2):
        turned = cells[128 * c : 128 * c + 128].T
        ref[0, :, 128 * c : 128 * c + 128] = turned[:blocks]
        ref[0, :, 128 * c + 256 : 128 * c + 384] = turned[blocks:]


def residual_kernel(head, cond, wet, less, span, own, flux, near_in, far_in, core, chip, table, resid_out, planes):
    (flux,) = balance(head, cond, own, (flux,), near_in, far_in, core, chip, table, planes)
    leave(resid_out, 4.0 * (less[...] + span[...] * wet[...]) - flux.reshape(256, 128))


def shape(*dims):
    return jax.ShapeDtypeStruct(dims, f32)


def call(kernel, outs, scratch, *operands, space=pltpu.VMEM, limit=vmem):
    whole = pl.BlockSpec(memory_space=space)
    return pl.pallas_call(
        kernel,
        out_shape=outs,
        in_specs=[whole] * len(operands),
        out_specs=[whole] * len(outs),
        scratch_shapes=scratch,
        compiler_params=pltpu.CompilerParams(vmem_limit_bytes=limit),
    )(*operands)


def exchange(near, far, core, chip):
    lateral, columns = lax.axis_size("dom"), lax.axis_size("depth")

    def swap(x, partner):
        places = [(t, d) for t in range(lateral) for d in range(columns)]
        pairs = []
        for t, d in places:
            u, e = partner(t, d)
            pairs.append((t * columns + d, u * columns + e))
        return lax.ppermute(x, ("dom", "depth"), pairs)

    def far_of(t, d):
        u = ((t + 1) ^ 1) - 1
        return (u, d) if 0 <= u < lateral else (t, d ^ 1)

    def chip_of(t, d):
        e = ((d + 1) ^ 1) - 1
        return (t, e) if 0 <= e < columns else (t ^ 1, d)

    far = swap(far, far_of)
    near = swap(near, lambda t, d: (t ^ 1, d))
    chip = swap(chip, chip_of)
    core = swap(core, lambda t, d: (t, d ^ 1))
    return near, far, core, chip


def pack(head, water_prev, alpha, shape_n, theta_r, theta_s, sat_cond, refine, destination):
    outs = [shape(rows, blocks, 128), shape(peers, chunk, 128), shape(blocks, 128)]
    scratch = [pltpu.SMEM((blocks,), jnp.int32)] * 2 + [pltpu.VMEM((1, blocks, 512), f32)] * 7
    scratch += [pltpu.VMEM((rows, blocks, 128), f32)]
    scratch += [pltpu.VMEM((2 * blocks * size, 128), f32) for size in (late, early)]
    scratch += [pltpu.VMEM((peers, 8, 128), f32), pltpu.VMEM((2 * blocks, 128), jnp.int32), pltpu.VMEM((blocks, 128), f32)]
    scratch += [pltpu.VMEM((blocks * late, 128), f32), pltpu.VMEM((blocks * early, 128), f32)]
    scratch += [pltpu.VMEM((384, 512), jnp.bfloat16)]
    scratch += [pltpu.VMEM((blocks, 128), jnp.int32), pltpu.SMEM((peers,), jnp.int32), pltpu.SMEM((blocks,), jnp.int32)]
    scratch += [pltpu.SemaphoreType.DMA((2,))]
    operands = (refine, destination, alpha, shape_n, sat_cond, theta_s, theta_r, head, water_prev)
    return call(pack_kernel, outs, scratch, *operands, space=pltpu.HBM, limit=64 * 1024 * 1024)


def on_device(head, water_prev, alpha, shape_n, theta_r, theta_s, sat_cond, refine, destination, neighbours):
    held, send, stay = pack(head, water_prev, alpha, shape_n, theta_r, theta_s, sat_cond, refine, destination)
    recv = lax.all_to_all(send, "dom", 0, 0, tiled=True, axis_index_groups=[sorted(range(peers), key=seat)])
    (settled,) = call(settle_kernel, [shape(fields, 256, 128)], [], held, stay)
    near = neighbours.reshape(blocks, 16).T
    near = jnp.concatenate([near, near], axis=1)
    cells, halo = shape(256, 128), [shape(64, 128)] * 4
    recv = recv.reshape(peers * chunk, 128)
    head, alpha, shape_n, sat, cond, wet, *outgoing = call(arrive_kernel, [cells] * 6 + halo, [], recv, settled)
    incoming = exchange(*outgoing)
    ghost = shape(2, 128, 128)
    sums = call(inside_kernel, [ghost, cells, cells], [], head, cond, near)
    less, span, water = call(later_kernel, [cells] * 3, [], recv, settled, wet)
    planes = [pltpu.VMEM((4, 256, 128), f32)]
    head, cond, wet, *outgoing = call(
        newton_kernel, [cells] * 3 + halo, planes, head, alpha, shape_n, sat, cond, span, water, *sums, *incoming, near
    )
    incoming = exchange(*outgoing)
    final = shape(1, blocks, 512)
    own, flux, new_head = call(last_inside_kernel, [ghost, cells, final], [], head, cond, near)
    (residual,) = call(residual_kernel, [final], planes, head, cond, wet, less, span, own, flux, *incoming, near)
    return new_head, residual


def solution(mesh):
    cells = P("depth", "dom", None)
    return jax.shard_map(
        on_device,
        mesh=mesh,
        in_specs=(cells,) * 7 + (P("dom"), P("dom"), P("dom", None, None)),
        out_specs=(cells, cells),
        check_vma=False,
    )
```

```python
import jax
import jax.numpy as jnp
from jax import lax
from jax.experimental import pallas as pl
from jax.experimental.pallas import tpu as pltpu
from jax.sharding import PartitionSpec as P

peers = 16
blocks = 64
fields = 6
room = 4
reach = 16
rows = fields * 4
late, early = 16, 8
chunk = room * rows + 8
vmem = 48 * 1024 * 1024
f32 = jnp.float32


def lane_take(x, index):
    numbers = lax.GatherDimensionNumbers((), (1,), (1,), (0,), (0,))
    return lax.gather(x, index[..., None], numbers, (1, 1), mode=lax.GatherScatterMode.PROMISE_IN_BOUNDS)


def row_take(x, index):
    numbers = lax.GatherDimensionNumbers((), (0,), (0,), (1,), (1,))
    return lax.gather(x, index[..., None], numbers, (1, 1), mode=lax.GatherScatterMode.PROMISE_IN_BOUNDS)


def seat(device):
    return peers - 1 - ((device & 3) * 4 + (device >> 2))


def iota(shape, axis):
    return lax.broadcasted_iota(jnp.int32, shape, axis)


def turn(x, shift, axis=None):
    axis = x.ndim - 1 if axis is None else axis
    shift = shift % x.shape[axis]
    if shift == 0:
        return x
    if x.ndim == 2:
        return pltpu.roll(x, shift, axis)
    flat = pltpu.roll(x.reshape(-1, x.shape[-1]), shift, 1)
    return flat.reshape(x.shape)


def plane_weights(bit_y, bit_z):
    source, fine = iota((128, 128), 0), iota((128, 128), 1)

    def line(bit, shift):
        coarse, index = (source >> shift) & 7, (fine >> shift) & 7
        near = 4 * bit + (index >> 1)
        far = jnp.clip(near + 2 * (index & 1) - 1, 0, 7)
        return jnp.where(coarse == near, 0.75, 0.0) + jnp.where(coarse == far, 0.25, 0.0)

    weight = line(bit_y, 3) * line(bit_z, 0)
    return jnp.where((source >> 6) == (fine >> 6), weight, 0.0).astype(jnp.bfloat16)


def pack_kernel(*refs):
    sources, targets, refs = refs[:9], refs[9:12], refs[12:]
    held, refs = refs[:9], refs[9:]
    own, part_late, part_early, part_place, places, stay, *refs = refs
    work_late, work_early, weights, flags, free, taken, sems = refs
    arriving = [pltpu.make_async_copy(source, ref, sems.at[0]) for source, ref in zip(sources, held)]
    for copy in arriving:
        copy.start()
    leaving = []

    def depart(source, target):
        copy = pltpu.make_async_copy(source, target, sems.at[1])
        copy.start()
        leaving.append(copy)

    for bits in range(4):
        table = plane_weights(bits // 2, bits % 2)
        for n in range(3):
            weights[128 * n : 128 * n + 128, 128 * bits : 128 * bits + 128] = table
    refine, destination = held[:2]
    me = lax.axis_index("dom")
    for peer in range(peers):
        free[peer] = jnp.where(peer == me, peers * room * late, seat(peer) * room * late)
        part_place[peer] = jnp.full((8, 128), -1.0, f32)
    places[...] = jnp.full((2 * blocks, 128), -1, jnp.int32)
    for copy in arriving:
        copy.wait()
    for block in range(blocks):
        flags[pl.ds(block, 1), :] = jnp.full((1, 128), refine[block], jnp.int32)
    lane = iota((blocks, 128), 1)
    half, fine_y, fine_z = (lane >> 6) & 1, (lane >> 3) & 7, lane & 7
    flag = flags[...]
    octant = jnp.maximum(flag - 1, 0)
    kept = flag == 0
    bit_x, bit_y, bit_z = (octant >> 2) & 1, (octant >> 1) & 1, octant & 1
    up_x = bit_x == 1

    def get(n):
        return [held[n][0, :, 128 * c : 128 * c + 128] for c in range(4)]

    plain_y, plain_z = 4 * bit_y + (fine_y >> 1), 4 * bit_z + (fine_z >> 1)
    inner = plain_y * 8 + plain_z
    plain_index = [jnp.where(kept, lane, parity * 64 + inner) for parity in range(2)]

    def plain(v):
        chosen = [
            jnp.where(up_x, v[2], v[0]),
            jnp.where(kept, v[1], jnp.where(up_x, v[2], v[0])),
            jnp.where(kept, v[2], jnp.where(up_x, v[3], v[1])),
            jnp.where(kept | up_x, v[3], v[1]),
        ]
        return [lane_take(chosen[c], plain_index[c % 2]) for c in range(4)]

    lower = lane < 64

    def smooth(v):
        r = [turn(x, 64) for x in v]
        base = [jnp.where(up_x, v[2 + c], v[c]) for c in range(2)]
        base_r = [jnp.where(up_x, r[2 + c], r[c]) for c in range(2)]
        near = [
            jnp.where(lower, base[0], base_r[0]),
            jnp.where(lower, base_r[0], base[0]),
            jnp.where(lower, base[1], base_r[1]),
            jnp.where(lower, base_r[1], base[1]),
        ]
        far = [
            jnp.where(lower, jnp.where(up_x, r[1], v[0]), base[0]),
            jnp.where(lower, base[0], jnp.where(up_x, r[3], r[1])),
            jnp.where(lower, base_r[0], base[1]),
            jnp.where(lower, base[1], jnp.where(up_x, v[3], r[2])),
        ]
        x = jnp.concatenate([0.75 * near[c] + 0.25 * far[c] for c in range(4)], axis=0)
        high = x.astype(jnp.bfloat16)
        x = x - high.astype(f32)
        middle = x.astype(jnp.bfloat16)
        x = (x - middle.astype(f32)).astype(jnp.bfloat16)
        y = jnp.dot(jnp.concatenate([high, middle, x], axis=1), weights[...], preferred_element_type=f32)
        result = []
        for c in range(4):
            parts = [y[blocks * c : blocks * (c + 1), 128 * n : 128 * n + 128] for n in range(4)]
            parts = [jnp.where(bit_z == 1, parts[n + 1], parts[n]) for n in (0, 2)]
            result.append(jnp.where(kept, v[c], jnp.where(bit_y == 1, parts[1], parts[0])))
        return result

    def keep(f, values, work, size, first):
        for c in range(4):
            own[f * 4 + c] = values[c]
            for g in range(blocks // 8):
                work[pl.ds(8 * g * size + (f - first) * 4 + c, 8, stride=size), :] = values[c][8 * g : 8 * g + 8]
        depart(own.at[4 * f : 4 * f + 4], targets[0].at[4 * f : 4 * f + 4])

    low = get(6)
    keep(0, smooth(get(7)), work_early, early, 0)
    keep(1, [x - y for x, y in zip(plain(low), smooth(get(8)))], work_early, early, 0)
    for n, f in ((2, 2), (3, 3), (4, 4)):
        keep(f, plain(get(n)), work_late, late, 2)
    high = get(5)
    keep(5, plain([x - y for x, y in zip(high, low)]), work_late, late, 2)

    for block in range(blocks):
        target = destination[block]
        owner = target >> 6
        row = free[owner]
        free[owner] = row + late
        taken[block] = row >> 1
        place = jnp.full((1, 128), target, jnp.int32)
        part_late[pl.ds(pl.multiple_of(row, late), late), :] = work_late[block * late : block * late + late, :]
        places[pl.ds(row >> 4, 1), :] = place
        stay[block : block + 1, :] = place.astype(f32)
    for peer in range(peers):
        part_place[peer, :room, :] = places[room * peer : room * peer + room, :].astype(f32)
    depart(part_late.reshape(2 * peers, room * late, 128).at[:peers], targets[1].at[:, : room * late])
    depart(part_place, targets[1].at[:, room * rows :])
    depart(stay, targets[2])

    for block in range(blocks):
        row = pl.multiple_of(taken[block], early)
        part_early[pl.ds(row, early), :] = work_early[block * early : block * early + early, :]
    depart(part_early.reshape(2 * peers, room * early, 128).at[:peers], targets[1].at[:, room * late : room * rows])
    for copy in leaving:
        copy.wait()


def find(places):
    position = lax.axis_index("dom") * blocks + (iota((blocks, 128), 1) & 63)
    hit = places.astype(jnp.int32) == position
    row = jnp.sum(jnp.where(hit, iota((blocks, 128), 0), 0), axis=0, keepdims=True)
    has = jnp.sum(jnp.where(hit, 1, 0), axis=0, keepdims=True) > 0
    return row + (iota((1, 128), 1) & 64), has


def settle_kernel(own, stay, out):
    index, _ = find(stay[...])
    index = jnp.broadcast_to(index, (128, 128))
    for f in range(fields):
        for c in range(2):
            cells = jnp.concatenate([own[f * 4 + c], own[f * 4 + c + 2]], axis=0).T
            out[f, 128 * c : 128 * c + 128, :] = lane_take(cells, index)


def closure(head, alpha, shape_n, cond):
    expo = 1.0 - 1.0 / shape_n
    log_t = shape_n * jnp.log(alpha * jnp.maximum(-head, 0.0))
    log_s = jnp.log(1.0 + jnp.exp(log_t))
    root = jnp.exp(-0.5 * expo * log_s)
    inner = 1.0 - jnp.exp(expo * (log_t - log_s))
    return cond * root * inner * inner, root * root


def cube(x):
    return x.reshape(4, 8, 8, 128)


def face_tiles(x):
    y0, y7 = x[:, 0], x[:, 7]
    return [
        x[0],
        turn(x[3], 64),
        jnp.concatenate([y0, turn(y0, 64)], axis=0),
        jnp.concatenate([y7, turn(y7, 64)], axis=0),
    ]


def pack_faces(head, cond):
    group = iota((8, 8, 128), 2) >> 4
    right = left = None
    for f in range(4):
        for q, x in enumerate((head, cond)):
            g = 2 * f + q
            if f < 2:
                part = turn(x[3 * f], 64 * f + g * reach)
            else:
                edge = x[:, 7 * (f - 2)]
                part = jnp.concatenate([turn(edge, g * reach), turn(edge, 64 + g * reach)], axis=0)
            left = part if left is None else jnp.where(group == g, part, left)
            right = part if right is None else jnp.where(group == (g + 3) % 8, part, right)
    return right.reshape(64, 128), left.reshape(64, 128)


def even(axis):
    return lax.axis_index(axis) % 2 == 0


def emit(head_ref, cond_ref, near, far, core, chip):
    right, left = pack_faces(cube(head_ref[...]), cube(cond_ref[...]))
    near[...] = jnp.where(even("dom"), right, left)
    far[...] = jnp.where(even("dom"), left, right)
    for q, ref in enumerate((head_ref, cond_ref)):
        top, bottom = ref[pl.ds(7, 32, stride=8), :], ref[pl.ds(0, 32, stride=8), :]
        core[32 * q : 32 * q + 32, :] = jnp.where(even("depth"), top, bottom)
        chip[32 * q : 32 * q + 32, :] = jnp.where(even("depth"), bottom, top)


def receive(recv, settled, chosen):
    def slots(start):
        return [recv[pl.ds(start(o), peers, stride=chunk), :] for o in range(room)]

    places = jnp.concatenate(slots(lambda o: room * rows + o), axis=0)
    index, has = find(places)
    index = jnp.broadcast_to(index, (128, 128))
    for f in chosen:
        halves = []
        for c in range(2):
            parts = []
            for r in (c, c + 2):
                if f < 2:
                    parts += slots(lambda o: room * late + o * early + f * 4 + r)
                else:
                    parts += slots(lambda o: o * late + (f - 2) * 4 + r)
            cells = jnp.concatenate(parts, axis=0).T
            halves.append(jnp.where(has, lane_take(cells, index), settled[f, 128 * c : 128 * c + 128, :]))
        yield jnp.concatenate(halves, axis=0)


def arrive_kernel(recv, settled, head_out, alpha_out, shape_out, sat_out, cond_out, wet_out, *outgoing):
    outs = (head_out, alpha_out, shape_out, sat_out)
    for ref, value in zip(outs, receive(recv, settled, (0, 2, 3, 4))):
        ref[...] = value
    cond_out[...], wet_out[...] = closure(*[ref[...] for ref in outs])
    emit(head_out, cond_out, *outgoing)


def later_kernel(recv, settled, wet, alpha, less_out, span_out, water_out, slope_out):
    for ref, value in zip((less_out, span_out), receive(recv, settled, (1, 5))):
        ref[...] = value
    water_out[...] = 4.0 * (less_out[...] + span_out[...] * wet[...])
    slope_out[...] = 4.0 * span_out[...] * alpha[...]


class Table:
    def __init__(self, values):
        lower = iota((8, 128), 1) < 64
        front = iota((8, 128), 0) < 4

        def row(f, e):
            return jnp.broadcast_to(values[4 * f + e : 4 * f + e + 1], (8, 128))

        self.one_x = jnp.where(lower, row(0, 0), row(1, 0))
        self.four_x = [
            jnp.where(
                lower,
                jnp.where(front, row(0, 2 * s), row(0, 2 * s + 1)),
                jnp.where(front, row(1, 2 * s), row(1, 2 * s + 1)),
            )
            for s in range(2)
        ]
        self.one_y = [row(f, 0) for f in (2, 3)]
        self.four_y = [
            jnp.where(
                lower,
                jnp.where(front, row(f, 0), row(f, 1)),
                jnp.where(front, row(f, 2), row(f, 3)),
            )
            for f in (2, 3)
        ]
        self.last_x = jnp.where(lower, row(0, 3), row(1, 3))
        self.last_y = [row(f, 3) for f in (2, 3)]


class Faces:
    def __init__(self, near):
        position = near[...] - lax.axis_index("dom") * blocks
        self.position, self.present = position, near[...] >= 0
        self.own = (position >= 0) & (position < blocks)
        there = Table(self.present.astype(jnp.int32))
        self.on_x, self.hang_x = there.one_x == 1, there.last_x == 1
        self.on_y, self.hang_y = [x == 1 for x in there.one_y], [x == 1 for x in there.last_y]

    def own_lanes(self):
        return Table(jnp.where(self.present & self.own, self.position, 0))

    def halo_lanes(self, q):
        group = ((iota((16, 128), 0) >> 2) ^ 1) * 2 + q
        right = group * reach + self.position - blocks
        left = ((group + 3) & 7) * reach + self.position + reach
        return Table(jnp.where(self.present & ~self.own, jnp.where(self.position < 0, left, right), 0))

    def away(self):
        table = Table((self.present & ~self.own).astype(jnp.int32))
        x = [jnp.where(self.hang_x, four, table.one_x) == 1 for four in table.four_x]
        y = [jnp.where(self.hang_y[n], table.four_y[n], table.one_y[n]) == 1 for n in range(2)]
        return x, y


def quarters(tile):
    pick = (iota((8, 128), 0) & 3) * 2
    result = []
    for a in range(4):
        pair = tile[2 * a] + tile[2 * a + 1]
        pair = 0.25 * (pair + turn(pair, 7, 0))
        result.append(row_take(pair, pick))
    return result


def ghosts(faces, table, tiles, coarse):
    low = iota((8, 128), 1) < 64
    alike = len(tiles) == 1
    made = []

    def both(lists, n, index):
        if alike:
            return lane_take(lists[0][n], index)
        return jnp.where(low, lane_take(lists[1][n], index), lane_take(lists[0][n], index))

    for a in range(8):
        one = both(tiles, a, table.one_x)
        four = both(coarse, a % 4, table.four_x[a // 4])
        made.append(jnp.where(faces.hang_x, four, one))
    for side, source in ((0, 0 if alike else 3), (1, 0 if alike else 2)):
        for a in range(4):
            index = table.one_y[side]
            one = jnp.where(low, lane_take(tiles[source][a], index), lane_take(tiles[source][a + 4], index))
            four = lane_take(coarse[source][a], table.four_y[side])
            made.append(jnp.where(faces.hang_y[side], four, one))
    return made


def own_ghosts(refs, near, out):
    faces = Faces(near)
    table = faces.own_lanes()
    for q, ref in enumerate(refs):
        tiles = face_tiles(cube(ref[...]))
        for n, value in enumerate(ghosts(faces, table, tiles, [quarters(tile) for tile in tiles])):
            out[q, 8 * n : 8 * n + 8, :] = value


def all_ghosts(faces, left, right, own):
    group = iota((8, 8, 128), 2) >> 4
    away_x, away_y = faces.away()
    for q in range(2):
        tile = jnp.where(group % 2 == q, right, left)
        made = ghosts(faces, faces.halo_lanes(q), [tile], [quarters(tile)])
        away = [away_x[0]] * 4 + [away_x[1]] * 4 + [away_y[0]] * 4 + [away_y[1]] * 4
        made = [jnp.where(far, x, own[q, 8 * n : 8 * n + 8, :]) for n, (far, x) in enumerate(zip(away, made))]
        yield jnp.stack(made[:8]), jnp.stack(made[8:12]), jnp.stack(made[12:])


def inside_kernel(head_ref, cond_ref, near, own, *outs):
    own_ghosts((head_ref, cond_ref), near, own)
    head, cond = cube(head_ref[...]), cube(cond_ref[...])
    lower = iota((8, 8, 128), 2) < 64
    level_k = iota((256, 128), 0) & 7

    def pair(k, other_k, h, other_h):
        face_k = k + other_k
        return face_k * (other_h - h), face_k

    def spread(below, above, sign):
        return [above[0]] + [above[n] + sign * below[n - 1] for n in range(1, len(above))] + [sign * below[-1]]

    steps = [pair(cond[n], cond[n + 1], head[n], head[n + 1]) for n in range(3)]
    cross = [jnp.where(lower, x, 0.0) for x in pair(cond[3], turn(cond[0], 64), head[3], turn(head[0], 64))]
    up_h, up_k = turn(head_ref[...], 255, 0), turn(cond_ref[...], 255, 0)
    rise = pair(cond_ref[...], up_k, head_ref[...], up_h + 1.0)
    rise = [jnp.where(level_k < 7, x, 0.0) for x in rise]
    along = pair(cond[:, :7], cond[:, 1:], head[:, :7], head[:, 1:])
    for q, (out, sign) in enumerate(zip(outs, (-1.0, 1.0))):
        x = spread([step[q] for step in steps], [step[q] for step in steps], sign)
        x[3] = x[3] + cross[q]
        x[0] = x[0] + sign * turn(cross[q], 64)
        empty = jnp.zeros((4, 1, 8, 128), f32)
        y = jnp.concatenate([along[q], empty], axis=1) + sign * jnp.concatenate([empty, along[q]], axis=1)
        z = rise[q] + sign * turn(rise[q], 1, 0)
        out[...] = (jnp.stack(x) + y).reshape(256, 128) + z


def last_inside_kernel(head_ref, cond_ref, near, own, flux_out, head_out):
    inside_kernel(head_ref, cond_ref, near, own, flux_out)
    leave(head_out, head_ref[...])


def balance(head_ref, cond_ref, own, sums_in, near_in, far_in, core, chip, near, planes):
    table = Faces(near)
    level = lax.axis_index("depth")
    head, cond = cube(head_ref[...]), cube(cond_ref[...])
    left = jnp.where(even("dom"), far_in[...], near_in[...]).reshape(8, 8, 128)
    right = jnp.where(even("dom"), near_in[...], far_in[...]).reshape(8, 8, 128)
    (around_h, *sides_h), (around_k, *sides_k) = all_ghosts(table, left, right, own)
    lower = iota((8, 8, 128), 2) < 64

    def term(on, k, other_k, h, other_h):
        face_k = jnp.where(on, k + other_k, 0.0)
        return jnp.where(on, face_k * (other_h - h), 0.0), face_k

    edge_k, edge_h = jnp.where(lower, cond[0], cond[3]), jnp.where(lower, head[0], head[3])
    x = term(table.on_x, edge_k, around_k, edge_h, around_h)
    y = [term(table.on_y[n], cond[:, j], sides_k[n], head[:, j], sides_h[n]) for n, j in ((0, 0), (1, 7))]
    below = jnp.where(even("depth"), chip[...], core[...])
    above = jnp.where(even("depth"), core[...], chip[...])
    last = lax.axis_size("depth") - 1
    for n, (plane, k, on, lift) in enumerate(((below, 0, level > 0, -1.0), (above, 7, level < last, 1.0))):
        own_h, own_k = head_ref[pl.ds(k, 32, stride=8), :], cond_ref[pl.ds(k, 32, stride=8), :]
        for q, value in enumerate(term(on, own_k, plane[32:], own_h, plane[:32] + lift)[: len(sums_in)]):
            planes[2 * n + q, pl.ds(k, 32, stride=8), :] = value
    level_k = iota((4, 8, 8, 128), 2)
    sums = []
    for q, ref in enumerate(sums_in):
        z = jnp.where(level_k == 0, cube(planes[q]), jnp.where(level_k == 7, cube(planes[2 + q]), 0.0))
        total = cube(ref[...]) + z
        slabs = [total[0] + jnp.where(lower, x[q], 0.0), total[1], total[2], total[3] + jnp.where(lower, 0.0, x[q])]
        total = jnp.stack(slabs)
        rows_j = [total[:, :1] + y[0][q][:, None], total[:, 1:7], total[:, 7:] + y[1][q][:, None]]
        sums.append(0.5 * jnp.concatenate(rows_j, axis=1))
    return sums


def newton_kernel(head, alpha, shape_n, sat, cond, slope, water, own, flux, total, *refs):
    incoming, (head_out, cond_out, wet_out, *outgoing), planes = refs[:5], refs[5:12], refs[12]
    flux, total = balance(head, cond, own, (flux, total), *incoming, planes)
    resid = cube(water[...]) - flux
    diagonal = cube(slope[...]) + total
    head_out[...] = (cube(head[...]) - resid / diagonal).reshape(256, 128)
    cond_out[...], wet_out[...] = closure(head_out[...], alpha[...], shape_n[...], sat[...])
    emit(head_out, cond_out, *outgoing)


def leave(ref, cells):
    for c in range(2):
        turned = cells[128 * c : 128 * c + 128].T
        ref[0, :, 128 * c : 128 * c + 128] = turned[:blocks]
        ref[0, :, 128 * c + 256 : 128 * c + 384] = turned[blocks:]


def residual_kernel(head, cond, wet, less, span, own, flux, near_in, far_in, core, chip, table, resid_out, planes):
    (flux,) = balance(head, cond, own, (flux,), near_in, far_in, core, chip, table, planes)
    leave(resid_out, 4.0 * (less[...] + span[...] * wet[...]) - flux.reshape(256, 128))


def shape(*dims):
    return jax.ShapeDtypeStruct(dims, f32)


def call(kernel, outs, scratch, *operands, space=pltpu.VMEM, limit=vmem):
    whole = pl.BlockSpec(memory_space=space)
    return pl.pallas_call(
        kernel,
        out_shape=outs,
        in_specs=[whole] * len(operands),
        out_specs=[whole] * len(outs),
        scratch_shapes=scratch,
        compiler_params=pltpu.CompilerParams(vmem_limit_bytes=limit),
    )(*operands)


def exchange(near, far, core, chip):
    lateral, columns = lax.axis_size("dom"), lax.axis_size("depth")

    def swap(x, partner):
        places = [(t, d) for t in range(lateral) for d in range(columns)]
        pairs = []
        for t, d in places:
            u, e = partner(t, d)
            pairs.append((t * columns + d, u * columns + e))
        return lax.ppermute(x, ("dom", "depth"), pairs)

    def far_of(t, d):
        u = ((t + 1) ^ 1) - 1
        return (u, d) if 0 <= u < lateral else (t, d ^ 1)

    def chip_of(t, d):
        e = ((d + 1) ^ 1) - 1
        return (t, e) if 0 <= e < columns else (t ^ 1, d)

    far = swap(far, far_of)
    near = swap(near, lambda t, d: (t ^ 1, d))
    chip = swap(chip, chip_of)
    core = swap(core, lambda t, d: (t, d ^ 1))
    return near, far, core, chip


def pack(head, water_prev, alpha, shape_n, theta_r, theta_s, sat_cond, refine, destination):
    outs = [shape(rows, blocks, 128), shape(peers, chunk, 128), shape(blocks, 128)]
    scratch = [pltpu.SMEM((blocks,), jnp.int32)] * 2 + [pltpu.VMEM((1, blocks, 512), f32)] * 7
    scratch += [pltpu.VMEM((rows, blocks, 128), f32)]
    scratch += [pltpu.VMEM((2 * blocks * size, 128), f32) for size in (late, early)]
    scratch += [pltpu.VMEM((peers, 8, 128), f32), pltpu.VMEM((2 * blocks, 128), jnp.int32), pltpu.VMEM((blocks, 128), f32)]
    scratch += [pltpu.VMEM((blocks * late, 128), f32), pltpu.VMEM((blocks * early, 128), f32)]
    scratch += [pltpu.VMEM((384, 512), jnp.bfloat16)]
    scratch += [pltpu.VMEM((blocks, 128), jnp.int32), pltpu.SMEM((peers,), jnp.int32), pltpu.SMEM((blocks,), jnp.int32)]
    scratch += [pltpu.SemaphoreType.DMA((2,))]
    operands = (refine, destination, alpha, shape_n, sat_cond, theta_s, theta_r, head, water_prev)
    return call(pack_kernel, outs, scratch, *operands, space=pltpu.HBM, limit=64 * 1024 * 1024)


def on_device(head, water_prev, alpha, shape_n, theta_r, theta_s, sat_cond, refine, destination, neighbours):
    held, send, stay = pack(head, water_prev, alpha, shape_n, theta_r, theta_s, sat_cond, refine, destination)
    recv = lax.all_to_all(send, "dom", 0, 0, tiled=True, axis_index_groups=[sorted(range(peers), key=seat)])
    (settled,) = call(settle_kernel, [shape(fields, 256, 128)], [], held, stay)
    near = neighbours.reshape(blocks, 16).T
    near = jnp.concatenate([near, near], axis=1)
    cells, halo = shape(256, 128), [shape(64, 128)] * 4
    recv = recv.reshape(peers * chunk, 128)
    head, alpha, shape_n, sat, cond, wet, *outgoing = call(arrive_kernel, [cells] * 6 + halo, [], recv, settled)
    incoming = exchange(*outgoing)
    ghost = shape(2, 128, 128)
    sums = call(inside_kernel, [ghost, cells, cells], [], head, cond, near)
    less, span, water, slope = call(later_kernel, [cells] * 4, [], recv, settled, wet, alpha)
    planes = [pltpu.VMEM((4, 256, 128), f32)]
    head, cond, wet, *outgoing = call(
        newton_kernel, [cells] * 3 + halo, planes, head, alpha, shape_n, sat, cond, slope, water, *sums, *incoming, near
    )
    incoming = exchange(*outgoing)
    final = shape(1, blocks, 512)
    own, flux, new_head = call(last_inside_kernel, [ghost, cells, final], [], head, cond, near)
    (residual,) = call(residual_kernel, [final], planes, head, cond, wet, less, span, own, flux, *incoming, near)
    return new_head, residual


def solution(mesh):
    cells = P("depth", "dom", None)
    return jax.shard_map(
        on_device,
        mesh=mesh,
        in_specs=(cells,) * 7 + (P("dom"), P("dom"), P("dom", None, None)),
        out_specs=(cells, cells),
        check_vma=False,
    )
```
